32 devices in a mesh: rows: 4 (over x, core), cols: 8 (over z, y).
Axes of the slice: x: 2, y: 2, z: 4, core: 2. Of those that a mesh axis runs over, the one named last changes fastest.
Arguments:
- blocks: bfloat16 [48, 48, 256, 256], P('rows', 'cols'), may hold values from -1.5 to 1.5
- pattern: int32 [48, 48], P('rows', 'cols'), may hold values 0 or 1
- pivot_inverse: bfloat16 [2, 256, 256], replicated, may hold values from -0.375 to 0.375
- right_sides: float32 [48, 3, 256], P('rows'), may hold values from -6 to 6
Outputs:
- factored: bfloat16 [48, 48, 256, 256], P('rows', 'cols')
- forward: float32 [48, 3, 256], P('rows')
The draws below stay inside these ranges and needn't reach their ends.
All inputs are finite; a program needn't handle non-finite values. No bound on the sum of `pattern` on one device may be relied on, other than what follows from the above.
Results may differ from the reference program's by a relative error of at most 0.0071.
Values may be sent and summed in bfloat16 or wider, within the bound.
No kernel may reach another device: no remote copies, remote signals or barrier semaphores. Data moves between devices by JAX's collectives and lax.ppermute only.
A program may use at most 128 MiB of HBM per device.

```python
import jax
import jax.numpy as jnp
from jax import lax

B = 256
DIRS = 3
CB = 6
RB = 12
NB = 48
N_ROWS = 4
N_COLS = 8


def touch_ends(values, stream_key, smallest, top_value):
    shape = values.shape
    index_at = [jax.random.randint(jax.random.fold_in(stream_key, axis), (), 0, shape[axis]) for axis in range(len(shape))]
    values = values.at[tuple(index_at)].set(smallest)
    longest = shape.index(max(shape))
    index_at[longest] = (index_at[longest] + 1) % shape[longest]
    return values.at[tuple(index_at)].set(top_value)


def levels(own_key, shape, pieces, least, largest):
    level, own = 1.0, jax.random.fold_in(own_key, 6)
    for position, parts in pieces:
        draws = jnp.exp(jax.random.uniform(jax.random.fold_in(own, position), (parts,), jnp.float32, least / len(pieces), largest / len(pieces)))
        level = level * jnp.repeat(draws, shape[position] // parts).reshape([-1 if axis == position else 1 for axis in range(len(shape))])
    return level


def scatter_about(stream_key, shape, deviation, most, shards=(), kind=jnp.bfloat16):
    entries = deviation * jax.random.normal(stream_key, shape, jnp.float32)
    if shards:
        entries = entries * levels(stream_key, shape, shards, -0.22, 0.18)
    return jnp.clip(entries, -most, most).astype(kind)


def setup_inputs(seed: int = 0) -> dict:
    seeds = jax.random.split(jax.random.key(seed), 5)
    blocks = scatter_about(seeds[0], (NB, NB, B, B), 0.25, 1.5, ((0, 4), (1, 8)))
    pattern = touch_ends((jax.random.randint(seeds[1], (NB, NB), 0, 2) < 1).astype(jnp.int32), jax.random.fold_in(seeds[1], 1), 0, 1)
    pivot_inverse = scatter_about(seeds[2], (2, B, B), B ** -0.5, 0.375)
    right_sides = scatter_about(seeds[3], (NB, DIRS, B), 1.0, 6.0, ((0, 4),), jnp.float32)
    return {"blocks": blocks, "pattern": pattern, "pivot_inverse": pivot_inverse, "right_sides": right_sides}


def reference(blocks, pattern, pivot_inverse, right_sides):
    glob = jnp.arange(NB)
    row_src = ((glob % N_ROWS) * RB + glob // N_ROWS).astype(jnp.int32)
    col_src = ((glob % N_COLS) * CB + glob // N_COLS).astype(jnp.int32)
    store = jnp.arange(NB)
    row_back = ((store % RB) * N_ROWS + store // RB).astype(jnp.int32)
    col_back = ((store % CB) * N_COLS + store // CB).astype(jnp.int32)
    live = pattern[row_src][:, col_src] == 1
    matrix = blocks[row_src][:, col_src]
    matrix = jnp.where(live[:, :, None, None], matrix, jnp.zeros((), blocks.dtype))
    rhs = right_sides[row_src]
    lowers = []
    for k in range(2):
        column = matrix[:, k].astype(jnp.float32)
        lower = jnp.einsum("nab,bc->nac", column, pivot_inverse[k].astype(jnp.float32)).astype(jnp.bfloat16)
        lower = jnp.where((glob > k)[:, None, None], lower, jnp.zeros((), jnp.bfloat16))
        upper = jnp.where((glob > k)[:, None, None], matrix[k], jnp.zeros((), jnp.bfloat16))
        upper_f = upper.astype(jnp.float32)

        def one_row(packed):
            arow, lrow, prow = packed
            prod = jnp.einsum("ab,jbc->jac", lrow.astype(jnp.float32), upper_f)
            fresh = (arow.astype(jnp.float32) - prod).astype(jnp.bfloat16)
            return jnp.where(prow[:, None, None], fresh, arow)

        matrix = lax.map(one_row, (matrix, lower, live))
        newcol = jnp.where((glob > k)[:, None, None], lower, matrix[:, k])
        matrix = matrix.at[:, k].set(newcol)
        lowers.append(lower)
    first = rhs[0]
    rhs = rhs - jnp.einsum("nab,cb->nca", lowers[0].astype(jnp.float32), first, precision=lax.Precision.HIGHEST)
    second = rhs[1]
    rhs = rhs - jnp.einsum("nab,cb->nca", lowers[1].astype(jnp.float32), second, precision=lax.Precision.HIGHEST)
    factored = matrix[row_back][:, col_back]
    return factored, rhs[row_back]
```

```python
import functools

import jax
import jax.numpy as jnp
from jax import lax
from jax.experimental import pallas as pl
from jax.experimental.pallas import tpu as pltpu
from jax.sharding import PartitionSpec as P

BF = jnp.bfloat16
F32 = jnp.float32
FLAG_ROWS = 16
PIECE_ROWS = 32
MOST_CHUNKS = 4
VMEM_LIMIT = 40 * 1024 * 1024


def broadcast_plan(groups):
    children = {g: [] for g in range(groups)}

    def hang(low, high, parent):
        if low < high:
            hub = (low + high) // 2
            children[parent].append(hub)
            hang(low, hub, hub)
            hang(hub + 1, high, hub)

    hang(1, groups, 0)
    depth = {0: 0}
    order = [0]
    for g in order:
        for child in children[g]:
            depth[child] = depth[g] + 1
            order.append(child)
    edges = [(g, child, 0) for g in order for child in children[g]]
    spare = {g: 2 - len(children[g]) for g in order}
    orphans = []
    for g in order:
        if spare[g]:
            edges.append((g, g, 1))
            spare[g] -= 1
        else:
            orphans.append(g)
    for g in orphans:
        helper = min((h for h in order if spare[h]), key=lambda h: (depth[h], -h))
        edges.append((helper, g, 1))
        spare[helper] -= 1
    colour = {}
    for start in range(len(edges)):
        if start in colour:
            continue
        colour[start] = 0
        stack = [start]
        while stack:
            e = stack.pop()
            for f in range(len(edges)):
                if f != e and f not in colour and (edges[f][0] == edges[e][0] or edges[f][1] == edges[e][1]):
                    colour[f] = 1 - colour[e]
                    stack.append(f)
    permutes = ([], [])
    own_from, other_from, other_depth = {0: 0}, {}, {}
    for e, (sender, receiver, cross) in enumerate(edges):
        for side in (0, 1):
            permutes[colour[e]].append((2 * sender + side, 2 * receiver + (side ^ cross)))
        if cross:
            other_from[receiver] = colour[e]
            other_depth[receiver] = depth[sender]
        else:
            own_from[receiver] = colour[e]
    return depth, own_from, other_depth, other_from, permutes


def dot(a, b):
    return jnp.dot(a, b, preferred_element_type=F32)


def dot_t(a, b):
    return lax.dot_general(a, b, (((1,), (1,)), ((), ())), preferred_element_type=F32)


def pieces_of(rows):
    n, w = rows.shape
    full = jnp.concatenate([rows, jnp.zeros((8 - n, w), F32)], 0) if n < 8 else rows
    high = full.astype(BF).astype(F32)
    middle = (full - high).astype(BF).astype(F32)
    low = full - high - middle
    return jnp.concatenate([high, middle, low, jnp.zeros((PIECE_ROWS - 24, w), F32)], 0).astype(BF)


def sum_pieces(x, n):
    return (x[0:8] + x[8:16] + x[16:24])[:n]


def prepare_kernel(chunk, pattern, column, row, rhs, column_out, row_out):
    rows, width = column.shape[0], column.shape[-1]
    cols = row.shape[1]
    lines = lax.broadcasted_iota(jnp.int32, (FLAG_ROWS, width), 0)
    for k in range(rows // chunk):
        flags = jnp.zeros((FLAG_ROWS, width), F32)
        for i in range(chunk):
            live = pattern[k * chunk + i, 0] == 1
            column_out[k, i * width : (i + 1) * width] = jnp.where(live, column[k * chunk + i, 0], jnp.zeros((), BF))
            flags = jnp.where((lines == i) & live, 1.0, flags)
        column_out[k, chunk * width : chunk * width + FLAG_ROWS] = flags.astype(BF)
    flags = jnp.zeros((FLAG_ROWS, width), F32)
    for j in range(cols):
        live = pattern[0, j] == 1
        row_out[j * width : (j + 1) * width] = jnp.where(live, row[0, j], jnp.zeros((), BF))
        flags = jnp.where((lines == j) & live, 1.0, flags)
    base = cols * width
    row_out[base : base + FLAG_ROWS] = flags.astype(BF)
    row_out[base + FLAG_ROWS : base + FLAG_ROWS + PIECE_ROWS] = pieces_of(rhs[0])


def prepare(blocks, pattern, right_sides, chunk):
    rows, cols, width, _ = blocks.shape
    dirs = right_sides.shape[1]
    n = rows // chunk
    return pl.pallas_call(
        functools.partial(prepare_kernel, chunk),
        grid=(1,),
        in_specs=[
            pl.BlockSpec(memory_space=pltpu.SMEM),
            pl.BlockSpec((rows, 1, width, width), lambda s: (0, 0, 0, 0)),
            pl.BlockSpec((1, cols, width, width), lambda s: (0, 0, 0, 0)),
            pl.BlockSpec((1, dirs, width), lambda s: (0, 0, 0)),
        ],
        out_specs=[
            pl.BlockSpec((n, chunk * width + FLAG_ROWS, width), lambda s: (0, 0, 0)),
            pl.BlockSpec((cols * width + FLAG_ROWS + PIECE_ROWS, width), lambda s: (0, 0)),
        ],
        out_shape=[
            jax.ShapeDtypeStruct((n, chunk * width + FLAG_ROWS, width), BF),
            jax.ShapeDtypeStruct((cols * width + FLAG_ROWS + PIECE_ROWS, width), BF),
        ],
        compiler_params=pltpu.CompilerParams(vmem_limit_bytes=VMEM_LIMIT),
    )(pattern, blocks, blocks, right_sides)


def panel_kernel(dirs, ncols, mine, other, corner, other_corner, inverse, upper, upper_one, sides):
    width = inverse.shape[-1]
    cols = upper.shape[0]
    even = lax.axis_index("rows") % 2 == 0
    col = lax.axis_index("cols")

    def pick(lo, hi):
        a, b = mine[lo:hi], other[lo:hi]
        return jnp.where(even, a, b), jnp.where(even, b, a)

    zero = jnp.zeros((), BF)
    upper_one[...] = jnp.where(even, corner[...], other_corner[...])
    lower_one = dot(jnp.where(even, other_corner[...], corner[...]), inverse[0]).astype(BF)
    base = cols * width
    flags = pick(base, base + FLAG_ROWS)[1].astype(F32)
    for j in range(cols):
        zeroth, first = pick(j * width, (j + 1) * width)
        zeroth = jnp.where(j * ncols + col > 0, zeroth, zero)
        fresh = (first.astype(F32) - dot(lower_one, zeroth)).astype(BF)
        keep = (flags[j : j + 1] > 0.5) & (j * ncols + col > 1)
        upper[j, 0:width] = zeroth
        upper[j, width : 2 * width] = jnp.where(keep, fresh, zero)
    side_zero, side_one = pick(base + FLAG_ROWS, base + FLAG_ROWS + PIECE_ROWS)
    sides[0] = side_zero
    later = sum_pieces(side_one.astype(F32), dirs) - sum_pieces(dot_t(side_zero, lower_one), dirs)
    sides[1] = pieces_of(later)


def panel(dirs, cols, ncols, mine, other, corner, other_corner, inverse):
    width = inverse.shape[-1]
    return pl.pallas_call(
        functools.partial(panel_kernel, dirs, ncols),
        out_shape=[
            jax.ShapeDtypeStruct((cols, 2 * width, width), BF),
            jax.ShapeDtypeStruct((width, width), BF),
            jax.ShapeDtypeStruct((2, PIECE_ROWS, width), BF),
        ],
        compiler_params=pltpu.CompilerParams(vmem_limit_bytes=VMEM_LIMIT),
        cost_estimate=pl.CostEstimate(
            flops=2 * (cols + 2) * width**3, bytes_accessed=8 * cols * width**2, transcendentals=0
        ),
    )(mine, other, corner, other_corner, inverse)


def update_kernel(chunk, index, nrows, ncols, sources, n_refs, aliased, *refs):
    pattern, blocks, rhs, upper, upper_one, sides, inverse = refs[:7]
    landed = refs[7 : 7 + n_refs]
    out, forward, columns, sems = refs[7 + n_refs + aliased :]
    width = inverse.shape[-1]
    cols = blocks.shape[1]
    row_device, col = lax.axis_index("rows"), lax.axis_index("cols")
    pair, side = col // 2, col % 2
    step = pl.program_id(0)

    @pl.when(step == 0)
    def _():
        for which in (0, 1):
            for ref, pairs in sources[which]:
                hit = functools.reduce(jnp.logical_or, [pair == g for g in pairs])
                source = landed[ref[0]] if ref[1] is None else landed[ref[0]].at[ref[1]]

                @pl.when(hit)
                def _(source=source, which=which):
                    place = side if which == 0 else 1 - side
                    pltpu.make_async_copy(source, columns.at[place], sems.at[which]).start()

        for which in (0, 1):
            pltpu.make_async_copy(columns.at[which], columns.at[which], sems.at[which]).wait()

    local = index * chunk + step
    here = local * nrows + row_device
    zero = jnp.zeros((), BF)
    at = pl.ds(pl.multiple_of(step * width, width), width)
    lower_zero = dot(columns[0, at], inverse[0]).astype(BF)
    lower_zero = jnp.where(here > 0, lower_zero, zero)
    flags = columns[1, chunk * width : chunk * width + FLAG_ROWS].astype(F32)
    lines = lax.broadcasted_iota(jnp.int32, flags.shape, 0)
    live = jnp.sum(jnp.where(lines == step, flags, 0.0), 0, keepdims=True) > 0.5
    pivot = (columns[1, at].astype(F32) - dot(lower_zero, upper_one[...])).astype(BF)
    lower_one = dot(jnp.where(live, pivot, zero), inverse[1]).astype(BF)
    lower_one = jnp.where(here > 1, lower_one, zero)
    lower = jnp.concatenate([lower_zero, lower_one], 1)
    for j in range(cols):
        keep = pattern[local, j] == 1

        @pl.when(keep)
        def _(j=j):
            out[0, j] = (blocks[0, j].astype(F32) - dot(lower, upper[j])).astype(BF)

        @pl.when(jnp.logical_not(keep))
        def _(j=j):
            out[0, j] = jnp.zeros((width, width), BF)

    @pl.when((col == 0) & (here > 0))
    def _():
        out[0, 0] = lower_zero

    @pl.when((col == 1) & (here > 1))
    def _():
        out[0, 0] = lower_one

    dirs = rhs.shape[1]
    first = rhs[0] - sum_pieces(dot_t(sides[0], lower_zero), dirs)
    forward[0] = first - sum_pieces(dot_t(sides[1], lower_one), dirs)


def update(chunk, index, nrows, ncols, sources, landed, pattern, blocks, rhs, upper, upper_one, sides, inverse, before):
    rows, cols, width, _ = blocks.shape
    dirs = rhs.shape[1]
    aliased = 0 if before is None else 2
    whole = pl.BlockSpec(memory_space=pltpu.VMEM)
    far = pl.BlockSpec(memory_space=pl.ANY)
    block_spec = pl.BlockSpec((1, cols, width, width), lambda s: (index * chunk + s, 0, 0, 0))
    rhs_spec = pl.BlockSpec((1, dirs, width), lambda s: (index * chunk + s, 0, 0))
    n_in = 7 + len(landed)
    return pl.pallas_call(
        functools.partial(update_kernel, chunk, index, nrows, ncols, sources, len(landed), aliased),
        grid=(chunk,),
        in_specs=[pl.BlockSpec(memory_space=pltpu.SMEM), block_spec, rhs_spec]
        + [whole] * 4
        + [far] * (len(landed) + aliased),
        out_specs=[block_spec, rhs_spec],
        out_shape=[jax.ShapeDtypeStruct(blocks.shape, BF), jax.ShapeDtypeStruct(rhs.shape, F32)],
        scratch_shapes=[
            pltpu.VMEM((2, chunk * width + FLAG_ROWS, width), BF),
            pltpu.SemaphoreType.DMA((2,)),
        ],
        input_output_aliases={n_in: 0, n_in + 1: 1} if aliased else {},
        compiler_params=pltpu.CompilerParams(vmem_limit_bytes=VMEM_LIMIT),
        cost_estimate=pl.CostEstimate(
            flops=4 * chunk * (cols + 2) * width**3, bytes_accessed=4 * chunk * (cols + 2) * width**2, transcendentals=0
        ),
    )(pattern, blocks, rhs, upper, upper_one, sides, inverse, *landed, *(before or ()))


def on_device(blocks, pattern, pivot_inverse, right_sides):
    rows, cols, width, _ = blocks.shape
    dirs = right_sides.shape[1]
    nrows = lax.axis_size("rows")
    ncols = lax.axis_size("cols")
    pair = lax.axis_index("cols") // 2
    side = lax.axis_index("cols") % 2
    row_device = lax.axis_index("rows")
    groups = ncols // 2
    depth, own_from, other_depth, other_from, permutes = broadcast_plan(groups)
    n = max(d for d in range(1, MOST_CHUNKS + 1) if rows % d == 0)
    chunk = rows // n
    columns, row = prepare(blocks, pattern, right_sides, chunk)

    def among(members):
        return functools.reduce(jnp.logical_or, [pair == g for g in members])

    def down_rows(x):
        reach = 1
        while reach < nrows // 2:
            hops = [(2 * h + s, 2 * (h + reach) + s) for h in range(min(reach, nrows // 2 - reach)) for s in (0, 1)]
            x = jnp.where(row_device < 2 * reach, x, lax.ppermute(x, "rows", hops))
            reach *= 2
        return x, lax.ppermute(x, "rows", [(r, r ^ 1) for r in range(nrows)])

    by_second = [g for g in range(1, groups) if own_from[g] == 1]
    deepest = max(other_depth.values())
    landed = []
    for step in range(n + deepest):
        payload = columns[step] if step < n else None
        if step:
            first, second = landed[step - 1]
            moved = jnp.where(among(by_second), second, first) if by_second else first
            payload = moved if payload is None else jnp.where(pair == 0, payload, moved)
        landed.append([lax.ppermute(payload, "cols", pairs) for pairs in permutes])

    mine, other = down_rows(row)

    def places(k):
        own, cross = {}, {}
        for g in range(groups):
            key = ("here",) if g == 0 else (own_from[g], k + depth[g] - 1)
            own.setdefault(key, []).append(g)
            cross.setdefault((other_from[g], k + other_depth[g]), []).append(g)
        return own, cross

    def array_at(key):
        return landed[key[1]][key[0]]

    own, cross = places(0)
    mine_first = columns[0, :width]
    for key, members in own.items():
        if key != ("here",):
            mine_first = jnp.where(among(members), array_at(key)[:width], mine_first)
    other_first = None
    for key, members in cross.items():
        piece = array_at(key)[:width]
        other_first = piece if other_first is None else jnp.where(among(members), piece, other_first)
    corner = jnp.where((side == 0) == (row_device == 1), mine_first, other_first)
    corner, other_corner = down_rows(corner)
    upper, upper_one, sides = panel(dirs, cols, ncols, mine, other, corner, other_corner, pivot_inverse)

    before = None
    for k in range(n):
        arrays, sources = [columns], []
        for which in places(k):
            found = []
            for key, members in which.items():
                if key == ("here",):
                    found.append(((0, k), members))
                else:
                    arrays.append(array_at(key))
                    found.append(((len(arrays) - 1, None), members))
            sources.append(found)
        before = update(
            chunk, k, nrows, ncols, sources, arrays, pattern, blocks, right_sides, upper, upper_one, sides,
            pivot_inverse, before,
        )
    return tuple(before)


def solution(mesh):
    return jax.shard_map(
        on_device,
        mesh=mesh,
        in_specs=(P("rows", "cols", None, None), P("rows", "cols"), P(), P("rows", None, None)),
        out_specs=(P("rows", "cols", None, None), P("rows", None, None)),
        check_vma=False,
    )
```

```python
import functools

import jax
import jax.numpy as jnp
from jax import lax
from jax.experimental import pallas as pl
from jax.experimental.pallas import tpu as pltpu
from jax.sharding import PartitionSpec as P

BF = jnp.bfloat16
F32 = jnp.float32
FLAG_ROWS = 16
PIECE_ROWS = 32
MOST_CHUNKS = 4
WIDE_VMEM = 56 * 1024 * 1024
VMEM_LIMIT = 20 * 1024 * 1024
EARLY_VMEM = 44 * 1024 * 1024
LATE_VMEM = 52 * 1024 * 1024


def broadcast_plan(groups):
    children = {g: [] for g in range(groups)}

    def hang(low, high, parent):
        if low < high:
            hub = (low + high) // 2
            children[parent].append(hub)
            hang(low, hub, hub)
            hang(hub + 1, high, hub)

    hang(1, groups, 0)
    depth = {0: 0}
    order = [0]
    for g in order:
        for child in children[g]:
            depth[child] = depth[g] + 1
            order.append(child)
    edges = [(g, child, 0) for g in order for child in children[g]]
    spare = {g: 2 - len(children[g]) for g in order}
    orphans = []
    for g in order:
        if spare[g]:
            edges.append((g, g, 1))
            spare[g] -= 1
        else:
            orphans.append(g)
    for g in orphans:
        helper = min((h for h in order if spare[h]), key=lambda h: (depth[h], -h))
        edges.append((helper, g, 1))
        spare[helper] -= 1
    colour = {}
    for start in range(len(edges)):
        if start in colour:
            continue
        colour[start] = 0
        stack = [start]
        while stack:
            e = stack.pop()
            for f in range(len(edges)):
                if f != e and f not in colour and (edges[f][0] == edges[e][0] or edges[f][1] == edges[e][1]):
                    colour[f] = 1 - colour[e]
                    stack.append(f)
    permutes = ([], [])
    own_from, other_from, other_depth = {0: 0}, {}, {}
    for e, (sender, receiver, cross) in enumerate(edges):
        for side in (0, 1):
            permutes[colour[e]].append((2 * sender + side, 2 * receiver + (side ^ cross)))
        if cross:
            other_from[receiver] = colour[e]
            other_depth[receiver] = depth[sender]
        else:
            own_from[receiver] = colour[e]
    return depth, own_from, other_depth, other_from, permutes


def dot(a, b):
    return jnp.dot(a, b, preferred_element_type=F32)


def dot_t(a, b):
    return lax.dot_general(a, b, (((1,), (1,)), ((), ())), preferred_element_type=F32)


def pieces_of(rows):
    n, w = rows.shape
    full = jnp.concatenate([rows, jnp.zeros((8 - n, w), F32)], 0) if n < 8 else rows
    high = full.astype(BF).astype(F32)
    middle = (full - high).astype(BF).astype(F32)
    low = full - high - middle
    return jnp.concatenate([high, middle, low, jnp.zeros((PIECE_ROWS - 24, w), F32)], 0).astype(BF)


def sum_pieces(x, n):
    return (x[0:8] + x[8:16] + x[16:24])[:n]


def prepare_kernel(chunk, pattern, column, row, rhs, *outs):
    *column_out, row_out = outs
    rows, width = column.shape[0], column.shape[-1]
    cols = row.shape[1]
    lines = lax.broadcasted_iota(jnp.int32, (FLAG_ROWS, width), 0)
    for k in range(rows // chunk):
        flags = jnp.zeros((FLAG_ROWS, width), F32)
        for i in range(chunk):
            live = pattern[0, k * chunk + i] == 1
            column_out[k][i * width : (i + 1) * width] = jnp.where(live, column[k * chunk + i, 0], jnp.zeros((), BF))
            flags = jnp.where((lines == i) & live, 1.0, flags)
        column_out[k][chunk * width : chunk * width + FLAG_ROWS] = flags.astype(BF)
    flags = jnp.zeros((FLAG_ROWS, width), F32)
    for j in range(cols):
        live = pattern[j, 0] == 1
        row_out[j * width : (j + 1) * width] = jnp.where(live, row[0, j], jnp.zeros((), BF))
        flags = jnp.where((lines == j) & live, 1.0, flags)
    base = cols * width
    row_out[base : base + FLAG_ROWS] = flags.astype(BF)
    row_out[base + FLAG_ROWS : base + FLAG_ROWS + PIECE_ROWS] = pieces_of(rhs[0])


def prepare(blocks, pattern, right_sides, chunk):
    rows, cols, width, _ = blocks.shape
    dirs = right_sides.shape[1]
    shapes = [(chunk * width + FLAG_ROWS, width)] * (rows // chunk)
    shapes.append((cols * width + FLAG_ROWS + PIECE_ROWS, width))
    return pl.pallas_call(
        functools.partial(prepare_kernel, chunk),
        grid=(1,),
        in_specs=[
            pl.BlockSpec(memory_space=pltpu.SMEM),
            pl.BlockSpec((rows, 1, width, width), lambda s: (0, 0, 0, 0)),
            pl.BlockSpec((1, cols, width, width), lambda s: (0, 0, 0, 0)),
            pl.BlockSpec((1, dirs, width), lambda s: (0, 0, 0)),
        ],
        out_specs=[pl.BlockSpec(shape, lambda s: (0, 0)) for shape in shapes],
        out_shape=[jax.ShapeDtypeStruct(shape, BF) for shape in shapes],
        compiler_params=pltpu.CompilerParams(vmem_limit_bytes=WIDE_VMEM),
    )(pattern, blocks, blocks, right_sides)


def panel_kernel(dirs, ncols, mine, other, corner, other_corner, inverse, upper, upper_one, sides):
    width = inverse.shape[-1]
    cols = upper.shape[1] // width
    even = lax.axis_index("rows") % 2 == 0
    col = lax.axis_index("cols")

    def pick(lo, hi):
        a, b = mine[lo:hi], other[lo:hi]
        return jnp.where(even, a, b), jnp.where(even, b, a)

    zero = jnp.zeros((), BF)
    upper_one[...] = jnp.where(even, corner[...], other_corner[...])
    lower_one = dot(jnp.where(even, other_corner[...], corner[...]), inverse[0]).astype(BF)
    base = cols * width
    flags = pick(base, base + FLAG_ROWS)[1].astype(F32)
    for j in range(cols):
        zeroth, first = pick(j * width, (j + 1) * width)
        zeroth = jnp.where(j * ncols + col > 0, zeroth, zero)
        fresh = (first.astype(F32) - dot(lower_one, zeroth)).astype(BF)
        keep = (flags[j : j + 1] > 0.5) & (j * ncols + col > 1)
        at = slice(j * width, (j + 1) * width)
        upper[0:width, at] = zeroth
        upper[width : 2 * width, at] = jnp.where(keep, fresh, zero)
    side_zero, side_one = pick(base + FLAG_ROWS, base + FLAG_ROWS + PIECE_ROWS)
    sides[0] = side_zero
    later = sum_pieces(side_one.astype(F32), dirs) - sum_pieces(dot_t(side_zero, lower_one), dirs)
    sides[1] = pieces_of(later)


def panel(dirs, cols, ncols, mine, other, corner, other_corner, inverse):
    width = inverse.shape[-1]
    return pl.pallas_call(
        functools.partial(panel_kernel, dirs, ncols),
        out_shape=[
            jax.ShapeDtypeStruct((2 * width, cols * width), BF),
            jax.ShapeDtypeStruct((width, width), BF),
            jax.ShapeDtypeStruct((2, PIECE_ROWS, width), BF),
        ],
        compiler_params=pltpu.CompilerParams(vmem_limit_bytes=VMEM_LIMIT),
        cost_estimate=pl.CostEstimate(
            flops=2 * (cols + 2) * width**3, bytes_accessed=8 * cols * width**2, transcendentals=0
        ),
    )(mine, other, corner, other_corner, inverse)


def update_kernel(chunk, first_chunk, nrows, ncols, sources, n_refs, aliased, *refs):
    pattern, blocks, rhs, upper, upper_one, sides, inverse = refs[:7]
    landed = refs[7 : 7 + n_refs]
    out, forward, columns, lower, work, in_sems, out_sems = refs[7 + n_refs + aliased :]
    width = inverse.shape[-1]
    count, cols = work.shape[:2]
    row_device, col = lax.axis_index("rows"), lax.axis_index("cols")
    pair, side = col // 2, col % 2
    zero = jnp.zeros((), BF)
    base = first_chunk * chunk
    tall = chunk * width

    def fetch(i):
        return pltpu.make_async_copy(blocks.at[base + i], work.at[i], in_sems.at[i])

    def send(i):
        return pltpu.make_async_copy(work.at[i], out.at[base + i], out_sems.at[i])

    @pl.loop(0, count)
    def _(i):
        fetch(i).start()

    for k, per_chunk in enumerate(sources):
        for which in (0, 1):
            for ref, pairs in per_chunk[which]:
                hit = functools.reduce(jnp.logical_or, [pair == g for g in pairs])

                @pl.when(hit)
                def _(source=landed[ref], which=which, k=k):
                    columns[k, side if which == 0 else 1 - side] = source[...]

    @pl.loop(0, len(sources))
    def _(k):
        start = (base + k * chunk) * nrows + row_device
        glob = start + nrows * (lax.broadcasted_iota(jnp.int32, (tall, 1), 0) // width)
        lower_zero = jnp.where(glob > 0, dot(columns[k, 0, 0:tall], inverse[0]), 0.0).astype(BF)
        lower[k, :, 0:width] = lower_zero
        pivot = (columns[k, 1, 0:tall].astype(F32) - dot(lower_zero, upper_one[...])).astype(BF)
        flags = columns[k, 1, tall : tall + FLAG_ROWS].astype(F32)
        kept = [jnp.where(flags[i : i + 1] > 0.5, pivot[i * width : (i + 1) * width], zero) for i in range(chunk)]
        lower_one = dot(jnp.concatenate(kept, 0), inverse[1])
        lower[k, :, width : 2 * width] = jnp.where(glob > 1, lower_one, 0.0).astype(BF)

    @pl.loop(0, count)
    def _(i):
        k, at = i // chunk, pl.ds(pl.multiple_of((i % chunk) * width, width), width)
        glob = (base + i) * nrows + row_device
        fetch(i).wait()
        change = dot(lower[k, at], upper[...])
        for j in range(cols):
            fresh = (work[i, j].astype(F32) - change[:, j * width : (j + 1) * width]).astype(BF)
            work[i, j] = jnp.where(pattern[j, base + i] == 1, fresh, zero)

        @pl.when((col == 0) & (glob > 0))
        def _():
            work[i, 0] = lower[k, at, 0:width]

        @pl.when((col == 1) & (glob > 1))
        def _():
            work[i, 0] = lower[k, at, width : 2 * width]

        send(i).start()
        dirs = rhs.shape[1]
        first = rhs[base + i] - sum_pieces(dot_t(sides[0], lower[k, at, 0:width]), dirs)
        forward[i] = first - sum_pieces(dot_t(sides[1], lower[k, at, width : 2 * width]), dirs)

    @pl.loop(0, count)
    def _(i):
        send(i).wait()


def update(
    chunk, first_chunk, nrows, ncols, sources, landed, pattern, blocks, rhs, upper, upper_one, sides, inverse, before, limit
):
    rows, cols, width, _ = blocks.shape
    dirs = rhs.shape[1]
    aliased = 0 if before is None else 1
    far = pl.BlockSpec(memory_space=pl.ANY)
    near = pl.BlockSpec(memory_space=pltpu.VMEM)
    count = chunk * len(sources)
    n_in = 7 + len(landed)
    return pl.pallas_call(
        functools.partial(update_kernel, chunk, first_chunk, nrows, ncols, sources, len(landed), aliased),
        in_specs=[pl.BlockSpec(memory_space=pltpu.SMEM), far] + [near] * (5 + len(landed)) + [far] * aliased,
        out_specs=[far, near],
        out_shape=[jax.ShapeDtypeStruct(blocks.shape, BF), jax.ShapeDtypeStruct((count, dirs, width), F32)],
        scratch_shapes=[
            pltpu.VMEM((len(sources), 2, chunk * width + FLAG_ROWS, width), BF),
            pltpu.VMEM((len(sources), chunk * width, 2 * width), BF),
            pltpu.VMEM((count, cols, width, width), BF),
            pltpu.SemaphoreType.DMA((count,)),
            pltpu.SemaphoreType.DMA((count,)),
        ],
        input_output_aliases={n_in: 0} if aliased else {},
        compiler_params=pltpu.CompilerParams(vmem_limit_bytes=limit),
        cost_estimate=pl.CostEstimate(
            flops=4 * count * (cols + 2) * width**3, bytes_accessed=4 * count * (cols + 2) * width**2, transcendentals=0
        ),
    )(pattern, blocks, rhs, upper, upper_one, sides, inverse, *landed, *(before or ()))


def on_device(blocks, pattern, pivot_inverse, right_sides):
    rows, cols, width, _ = blocks.shape
    dirs = right_sides.shape[1]
    nrows = lax.axis_size("rows")
    ncols = lax.axis_size("cols")
    pair = lax.axis_index("cols") // 2
    side = lax.axis_index("cols") % 2
    row_device = lax.axis_index("rows")
    groups = ncols // 2
    depth, own_from, other_depth, other_from, permutes = broadcast_plan(groups)
    n = max(d for d in range(1, MOST_CHUNKS + 1) if rows % d == 0)
    chunk = rows // n
    pattern = pattern.T
    *columns, row = prepare(blocks, pattern, right_sides, chunk)

    def among(members):
        return functools.reduce(jnp.logical_or, [pair == g for g in members])

    def down_rows(x):
        reach = 1
        while reach < nrows // 2:
            hops = [(2 * h + s, 2 * (h + reach) + s) for h in range(min(reach, nrows // 2 - reach)) for s in (0, 1)]
            x = jnp.where(row_device < 2 * reach, x, lax.ppermute(x, "rows", hops))
            reach *= 2
        return x, lax.ppermute(x, "rows", [(r, r ^ 1) for r in range(nrows)])

    by_second = [g for g in range(1, groups) if own_from[g] == 1]
    deepest = max(other_depth.values())
    landed = []
    for step in range(n + deepest):
        payload = columns[step] if step < n else None
        if step:
            first, second = landed[step - 1]
            moved = jnp.where(among(by_second), second, first) if by_second else first
            payload = moved if payload is None else jnp.where(pair == 0, payload, moved)
        landed.append([lax.ppermute(payload, "cols", pairs) for pairs in permutes])

    mine, other = down_rows(row)

    def places(k):
        own, cross = {}, {}
        for g in range(groups):
            key = ("here",) if g == 0 else (own_from[g], k + depth[g] - 1)
            own.setdefault(key, []).append(g)
            cross.setdefault((other_from[g], k + other_depth[g]), []).append(g)
        return own, cross

    def array_at(key):
        return landed[key[1]][key[0]]

    own, cross = places(0)
    mine_first = columns[0][:width]
    for key, members in own.items():
        if key != ("here",):
            mine_first = jnp.where(among(members), array_at(key)[:width], mine_first)
    other_first = None
    for key, members in cross.items():
        piece = array_at(key)[:width]
        other_first = piece if other_first is None else jnp.where(among(members), piece, other_first)
    corner = jnp.where((side == 0) == (row_device == 1), mine_first, other_first)
    corner, other_corner = down_rows(corner)
    upper, upper_one, sides = panel(dirs, cols, ncols, mine, other, corner, other_corner, pivot_inverse)

    out, forward = None, []
    for first_chunk, last_chunk, limit in ((0, n - 1, EARLY_VMEM), (n - 1, n, LATE_VMEM)):
        arrays, sources = [], []
        for k in range(first_chunk, last_chunk):
            sources.append([])
            for which in places(k):
                found = []
                for key, members in which.items():
                    found.append((len(arrays), members))
                    arrays.append(columns[k] if key == ("here",) else array_at(key))
                sources[-1].append(found)
        if sources:
            out, part = update(
                chunk, first_chunk, nrows, ncols, sources, arrays, pattern, blocks, right_sides, upper, upper_one, sides,
                pivot_inverse, None if out is None else (out,), limit,
            )
            forward.append(part)
    return out, jnp.concatenate(forward, 0)


def solution(mesh):
    return jax.shard_map(
        on_device,
        mesh=mesh,
        in_specs=(P("rows", "cols", None, None), P("rows", "cols"), P(), P("rows", None, None)),
        out_specs=(P("rows", "cols", None, None), P("rows", None, None)),
        check_vma=False,
    )
```

```python
import functools

import jax
import jax.numpy as jnp
from jax import lax
from jax.experimental import pallas as pl
from jax.experimental.pallas import tpu as pltpu
from jax.sharding import PartitionSpec as P

BF = jnp.bfloat16
F32 = jnp.float32
FLAG_ROWS = 16
PIECE_ROWS = 32
MOST_CHUNKS = 3
BATCH = 3
WIDE_VMEM = 54 * 1024 * 1024
VMEM_LIMIT = 20 * 1024 * 1024
UPDATE_VMEM = 44 * 1024 * 1024


def broadcast_plan(groups):
    children = {g: [] for g in range(groups)}

    def hang(low, high, parent):
        if low < high:
            hub = (low + high) // 2
            children[parent].append(hub)
            hang(low, hub, hub)
            hang(hub + 1, high, hub)

    hang(1, groups, 0)
    depth = {0: 0}
    order = [0]
    for g in order:
        for child in children[g]:
            depth[child] = depth[g] + 1
            order.append(child)
    edges = [(g, child, 0) for g in order for child in children[g]]
    spare = {g: 2 - len(children[g]) for g in order}
    orphans = []
    for g in order:
        if spare[g]:
            edges.append((g, g, 1))
            spare[g] -= 1
        else:
            orphans.append(g)
    for g in orphans:
        helper = min((h for h in order if spare[h]), key=lambda h: (depth[h], -h))
        edges.append((helper, g, 1))
        spare[helper] -= 1
    colour = {}
    for start in range(len(edges)):
        if start in colour:
            continue
        colour[start] = 0
        stack = [start]
        while stack:
            e = stack.pop()
            for f in range(len(edges)):
                if f != e and f not in colour and (edges[f][0] == edges[e][0] or edges[f][1] == edges[e][1]):
                    colour[f] = 1 - colour[e]
                    stack.append(f)
    permutes = ([], [])
    own_from, other_from, other_depth = {0: 0}, {}, {}
    for e, (sender, receiver, cross) in enumerate(edges):
        for side in (0, 1):
            permutes[colour[e]].append((2 * sender + side, 2 * receiver + (side ^ cross)))
        if cross:
            other_from[receiver] = colour[e]
            other_depth[receiver] = depth[sender]
        else:
            own_from[receiver] = colour[e]
    return depth, own_from, other_depth, other_from, permutes


def dot(a, b):
    return jnp.dot(a, b, preferred_element_type=F32)


def dot_t(a, b):
    return lax.dot_general(a, b, (((1,), (1,)), ((), ())), preferred_element_type=F32)


def pieces_of(rows):
    n, w = rows.shape
    full = jnp.concatenate([rows, jnp.zeros((8 - n, w), F32)], 0) if n < 8 else rows
    high = full.astype(BF).astype(F32)
    middle = (full - high).astype(BF).astype(F32)
    low = full - high - middle
    return jnp.concatenate([high, middle, low, jnp.zeros((PIECE_ROWS - 24, w), F32)], 0).astype(BF)


def sum_pieces(x, n):
    return (x[0:8] + x[8:16] + x[16:24])[:n]


def slots_of(rows):
    return max(1, rows * 5 // 6)


def chunk_height(rows, width, n):
    return -(-(FLAG_ROWS + slots_of(rows) * width) // (16 * n)) * 16


def pack_kernel(n, height, pattern, column, first_out, later_out, rest_out, packed):
    rows, width = column.shape[0], column.shape[-1]
    slots = slots_of(rows)
    zero = jnp.zeros((), BF)
    lines = lax.broadcasted_iota(jnp.int32, (FLAG_ROWS, width), 0)
    flags = jnp.zeros((FLAG_ROWS, width), F32)
    place = jnp.int32(0)
    for i in range(rows):
        live = pattern[0, i] == 1
        occupied = live | (lax.axis_index("rows") < 2) if i == 0 else live
        start = jnp.where(place < slots, FLAG_ROWS + place * width, n * height + (place - slots) * width)

        @pl.when(occupied)
        def _(i=i, live=live, start=start):
            packed[pl.ds(pl.multiple_of(start, 16), width)] = jnp.where(live, column[i, 0], zero)

        flags = jnp.where((lines == i) & occupied, 1.0, flags)
        place = place + occupied.astype(jnp.int32)
    packed[0:FLAG_ROWS] = flags.astype(BF)
    first_out[...] = packed[0:height]
    for k in range(1, n):
        later_out[k - 1] = packed[k * height : (k + 1) * height]
    rest_out[...] = packed[n * height :]


def pack(blocks, pattern, n, height):
    rows, cols, width, _ = blocks.shape
    rest = (rows - slots_of(rows)) * width
    shapes = [(height, width), (n - 1, height, width), (rest, width)]
    near = pl.BlockSpec(memory_space=pltpu.VMEM)
    return pl.pallas_call(
        functools.partial(pack_kernel, n, height),
        grid=(1,),
        in_specs=[
            pl.BlockSpec(memory_space=pltpu.SMEM),
            pl.BlockSpec((rows, 1, width, width), lambda s: (0, 0, 0, 0)),
        ],
        out_specs=[near] * 3,
        out_shape=[jax.ShapeDtypeStruct(shape, BF) for shape in shapes],
        scratch_shapes=[pltpu.VMEM((n * height + rest, width), BF)],
        compiler_params=pltpu.CompilerParams(vmem_limit_bytes=WIDE_VMEM),
    )(pattern, blocks)


def row_kernel(pattern, row, rhs, out):
    cols, width = row.shape[1], row.shape[-1]
    lines = lax.broadcasted_iota(jnp.int32, (FLAG_ROWS, width), 0)
    flags = jnp.zeros((FLAG_ROWS, width), F32)
    for j in range(cols):
        live = pattern[j, 0] == 1
        out[j * width : (j + 1) * width] = jnp.where(live, row[0, j], jnp.zeros((), BF))
        flags = jnp.where((lines == j) & live, 1.0, flags)
    base = cols * width
    out[base : base + FLAG_ROWS] = flags.astype(BF)
    out[base + FLAG_ROWS : base + FLAG_ROWS + PIECE_ROWS] = pieces_of(rhs[0])


def pack_row(blocks, pattern, right_sides):
    rows, cols, width, _ = blocks.shape
    dirs = right_sides.shape[1]
    shape = (cols * width + FLAG_ROWS + PIECE_ROWS, width)
    return pl.pallas_call(
        row_kernel,
        grid=(1,),
        in_specs=[
            pl.BlockSpec(memory_space=pltpu.SMEM),
            pl.BlockSpec((1, cols, width, width), lambda s: (0, 0, 0, 0)),
            pl.BlockSpec((1, dirs, width), lambda s: (0, 0, 0)),
        ],
        out_specs=pl.BlockSpec(shape, lambda s: (0, 0)),
        out_shape=jax.ShapeDtypeStruct(shape, BF),
        compiler_params=pltpu.CompilerParams(vmem_limit_bytes=WIDE_VMEM),
    )(pattern, blocks, right_sides)


def pick_kernel(tests, places, start, height, *refs):
    sources, out = refs[: len(tests)], refs[-1]
    row_device, col = lax.axis_index("rows"), lax.axis_index("cols")
    for test, place, source in zip(tests, places, sources):

        @pl.when(test(row_device, col))
        def _(place=place, source=source):
            at = slice(start, start + height)
            out[...] = source[at] if place is None else source[place, at]


def pick(choices, start=0, height=None, after=()):
    tests, arrays, places = zip(*((t, *a) if isinstance(a, tuple) else (t, a, None) for t, a in choices))
    height = height or arrays[0].shape[-2]
    after = [a for a in after if all(a is not b for b in arrays)]
    near = pl.BlockSpec(memory_space=pltpu.VMEM)
    return pl.pallas_call(
        functools.partial(pick_kernel, tests, places, start, height),
        in_specs=[near] * len(arrays) + [pl.BlockSpec(memory_space=pl.ANY)] * len(after),
        out_specs=near,
        out_shape=jax.ShapeDtypeStruct((height, arrays[0].shape[-1]), BF),
        compiler_params=pltpu.CompilerParams(vmem_limit_bytes=VMEM_LIMIT),
    )(*arrays, *after)


def corner_kernel(own_tests, cross_tests, slots, *refs):
    sources, out, counts = refs[: len(own_tests) + len(cross_tests)], refs[-2], refs[-1]
    width = out.shape[0] - FLAG_ROWS
    row_device, col = lax.axis_index("rows"), lax.axis_index("cols")
    own_side = (col % 2 == 0) == (row_device % 2 == 1)
    counts[...] = jnp.zeros(counts.shape, F32)
    for k, (test, source) in enumerate(zip(own_tests + cross_tests, sources)):
        wanted = own_side if k < len(own_tests) else jnp.logical_not(own_side)

        @pl.when(test(row_device, col))
        def _(source=source, wanted=wanted):
            taken = jnp.sum(source[0:FLAG_ROWS].astype(F32), 0, keepdims=True)
            counts[...] = jnp.maximum(counts[...], taken)

            @pl.when(wanted)
            def _():
                out[0:width] = source[FLAG_ROWS : FLAG_ROWS + width]

    out[width:] = jnp.where(counts[0:FLAG_ROWS] > slots, 1.0, 0.0).astype(BF)


def corner_of(own, cross, slots, width):
    near = pl.BlockSpec(memory_space=pltpu.VMEM)
    own_tests, cross_tests = [t for t, _ in own], [t for t, _ in cross]
    return pl.pallas_call(
        functools.partial(corner_kernel, own_tests, cross_tests, slots),
        in_specs=[near] * len(own + cross),
        out_specs=near,
        out_shape=jax.ShapeDtypeStruct((width + FLAG_ROWS, width), BF),
        scratch_shapes=[pltpu.VMEM((FLAG_ROWS, width), F32)],
        compiler_params=pltpu.CompilerParams(vmem_limit_bytes=VMEM_LIMIT),
    )(*[a for _, a in own + cross])


def merge_kernel(bound, mine, moved, out):
    width = out.shape[0] - FLAG_ROWS
    keep = lax.axis_index("rows") < bound
    out[0:width] = jnp.where(keep, mine[0:width], moved[0:width])
    out[width:] = jnp.maximum(mine[width:].astype(F32), moved[width:].astype(F32)).astype(BF)


def merge(bound, mine, moved):
    near = pl.BlockSpec(memory_space=pltpu.VMEM)
    return pl.pallas_call(
        functools.partial(merge_kernel, bound),
        in_specs=[near] * 2,
        out_specs=near,
        out_shape=jax.ShapeDtypeStruct(mine.shape, BF),
        compiler_params=pltpu.CompilerParams(vmem_limit_bytes=VMEM_LIMIT),
    )(mine, moved)


def panel_kernel(dirs, ncols, mine, other, corner, other_corner, inverse, upper, upper_one, sides, over):
    width = inverse.shape[-1]
    cols = upper.shape[1] // width
    even = lax.axis_index("rows") % 2 == 0
    col = lax.axis_index("cols")

    def pick(lo, hi):
        a, b = mine[lo:hi], other[lo:hi]
        return jnp.where(even, a, b), jnp.where(even, b, a)

    zero = jnp.zeros((), BF)
    over[...] = jnp.maximum(corner[width:].astype(F32), other_corner[width:].astype(F32))[:, 0:128]
    upper_one[...] = jnp.where(even, corner[0:width], other_corner[0:width])
    lower_one = dot(jnp.where(even, other_corner[0:width], corner[0:width]), inverse[0]).astype(BF)
    base = cols * width
    flags = pick(base, base + FLAG_ROWS)[1].astype(F32)
    for j in range(cols):
        zeroth, first = pick(j * width, (j + 1) * width)
        zeroth = jnp.where(j * ncols + col > 0, zeroth, zero)
        fresh = (first.astype(F32) - dot(lower_one, zeroth)).astype(BF)
        keep = (flags[j : j + 1] > 0.5) & (j * ncols + col > 1)
        at = slice(j * width, (j + 1) * width)
        upper[0:width, at] = zeroth
        upper[width : 2 * width, at] = jnp.where(keep, fresh, zero)
    side_zero, side_one = pick(base + FLAG_ROWS, base + FLAG_ROWS + PIECE_ROWS)
    sides[0] = side_zero
    later = sum_pieces(side_one.astype(F32), dirs) - sum_pieces(dot_t(side_zero, lower_one), dirs)
    sides[1] = pieces_of(later)


def panel(dirs, cols, ncols, mine, other, corner, other_corner, inverse):
    width = inverse.shape[-1]
    return pl.pallas_call(
        functools.partial(panel_kernel, dirs, ncols),
        out_shape=[
            jax.ShapeDtypeStruct((2 * width, cols * width), BF),
            jax.ShapeDtypeStruct((width, width), BF),
            jax.ShapeDtypeStruct((2, PIECE_ROWS, width), BF),
            jax.ShapeDtypeStruct((FLAG_ROWS, 128), F32),
        ],
        compiler_params=pltpu.CompilerParams(vmem_limit_bytes=VMEM_LIMIT),
        cost_estimate=pl.CostEstimate(
            flops=2 * (cols + 2) * width**3, bytes_accessed=8 * cols * width**2, transcendentals=0
        ),
    )(mine, other, corner, other_corner, inverse)


def update_kernel(n, height, nrows, ncols, sources, n_refs, last, *refs):
    pattern, blocks = refs[:2]
    given, landed, extra = refs[2:7], refs[7 : 7 + n_refs], refs[7 + n_refs : 10 + n_refs]
    outs = refs[7 + n_refs + (4 if last else 1) :]
    out, forward = outs[:2]
    scratch = outs[2 if last else 3 :]
    columns, lower, work, flags_v, flags_s, slot_of, order, in_sems, out_sems, flag_sem = scratch[:10]
    row_device, col = lax.axis_index("rows"), lax.axis_index("cols")
    pair, side = col // 2, col % 2
    zero = jnp.zeros((), BF)
    rows, cols, width = work.shape[:3]
    slots = slots_of(rows)

    copies = []
    if last:
        near, given_sems, column_sems = scratch[10:15], scratch[15], scratch[16]
        rest_own, rest_cross, done = extra
        tail = slice(n * height, None)
        moves = list(zip(given, near)) + [(done, forward)]
        moves += [(rest_own, columns.at[side, tail]), (rest_cross, columns.at[1 - side, tail])]
        for m, (source, target) in enumerate(moves):
            copies.append(pltpu.make_async_copy(source, target, given_sems.at[m]))
            copies[-1].start()
    else:
        near = given
        outs[2][...] = extra[0][...]
    rhs, upper, upper_one, sides, inverse = near

    for k, per_chunk in enumerate(sources):
        for which in (0, 1):
            for ref, pairs in per_chunk[which]:
                hit = functools.reduce(jnp.logical_or, [pair == g for g in pairs])

                @pl.when(hit)
                def _(source=landed[ref[0]], place=ref[1], which=which, k=k):
                    source = source if place is None else source.at[place]
                    at = slice(k * height, (k + 1) * height)
                    target = columns.at[side if which == 0 else 1 - side, at]
                    if last:
                        pltpu.make_async_copy(source, target, column_sems.at[k, which]).start()
                    else:
                        target[...] = source[...]

    if last:
        for copy in copies:
            copy.wait()
        for k in range(n):
            for which in (0, 1):
                at = slice(k * height, (k + 1) * height)
                target = columns.at[side if which == 0 else 1 - side, at]
                pltpu.make_async_copy(target, target, column_sems.at[k, which]).wait()

    for b in (0, 1):
        flags_v[b * FLAG_ROWS : (b + 1) * FLAG_ROWS] = columns[b, 0:FLAG_ROWS].astype(F32)[:, 0:128].astype(jnp.int32)
    copy = pltpu.make_async_copy(flags_v, flags_s, flag_sem)
    copy.start()
    copy.wait()

    early = ((n - 1) * height - FLAG_ROWS) // width
    zeroth = first = count = jnp.int32(0)
    for i in range(rows):
        occupied = flags_s[i, 0], flags_s[FLAG_ROWS + i, 0]
        slot_zeroth, slot_first = jnp.where(occupied[0] > 0, zeroth, -1), jnp.where(occupied[1] > 0, first, -1)
        slot_of[0, i] = slot_zeroth
        slot_of[1, i] = slot_first
        ready = (slot_zeroth < early) & (slot_first < early)
        mine = jnp.logical_not(ready) if last else ready
        order[count] = i
        count = count + mine.astype(jnp.int32)
        zeroth, first = zeroth + occupied[0], first + occupied[1]

    def row_at(t):
        return order[jnp.minimum(t, count - 1)]

    def fetch(t):
        return pltpu.make_async_copy(blocks.at[row_at(t)], work.at[t], in_sems.at[t])

    def send(t):
        return pltpu.make_async_copy(work.at[t], out.at[row_at(t)], out_sems.at[t])

    @pl.loop(0, count)
    def _(t):
        fetch(t).start()

    if not last:
        forward[...] = rhs[...]

    def block_at(b, i):
        slot = slot_of[b, i]
        start = jnp.where(slot < slots, FLAG_ROWS + slot * width, n * height + (slot - slots) * width)
        start = jnp.where(slot < 0, 0, start)
        return jnp.where(slot >= 0, columns[b, pl.ds(pl.multiple_of(start, 16), width)], zero)

    @pl.loop(0, (count + BATCH - 1) // BATCH)
    def _(g):
        members = [row_at(g * BATCH + t) for t in range(BATCH)]
        globs = [i * nrows + row_device for i in members]
        parts = [slice(t * width, (t + 1) * width) for t in range(BATCH)]
        product = dot(jnp.concatenate([block_at(0, i) for i in members], 0), inverse[0])
        lower_zero = jnp.concatenate(
            [jnp.where(glob > 0, product[at], 0.0).astype(BF) for glob, at in zip(globs, parts)], 0
        )
        change = dot(lower_zero, upper_one[...])
        pivots = []
        for i, at in zip(members, parts):
            fresh = (block_at(1, i).astype(F32) - change[at]).astype(BF)
            pivots.append(jnp.where(slot_of[1, i] >= 0, fresh, zero))
        product = dot(jnp.concatenate(pivots, 0), inverse[1])
        for t, (glob, at) in enumerate(zip(globs, parts)):
            lower[g * BATCH + t, :, 0:width] = lower_zero[at]
            lower[g * BATCH + t, :, width : 2 * width] = jnp.where(glob > 1, product[at], 0.0).astype(BF)

    @pl.loop(0, count)
    def _(t):
        i = row_at(t)
        glob = i * nrows + row_device
        dirs = rhs.shape[1]
        fetch(t).wait()
        head = rhs[i] - sum_pieces(dot_t(sides[0], lower[t, :, 0:width]), dirs)
        forward[i] = head - sum_pieces(dot_t(sides[1], lower[t, :, width : 2 * width]), dirs)
        lower_zeroth = (col == 0) & (glob > 0)
        lower_first = (col == 1) & (glob > 1)
        for j in range(cols):
            change = dot(lower[t], upper[:, j * width : (j + 1) * width])
            fresh = (work[t, j].astype(F32) - change).astype(BF)
            fresh = jnp.where(pattern[j, i] == 1, fresh, zero)
            if j == 0:
                fresh = jnp.where(lower_zeroth, lower[t, :, 0:width], fresh)
                fresh = jnp.where(lower_first, lower[t, :, width : 2 * width], fresh)
            work[t, j] = fresh
        send(t).start()

    @pl.loop(0, count)
    def _(t):
        send(t).wait()


def update(n, height, nrows, ncols, sources, landed, pattern, blocks, given, extra, last):
    rows, cols, width, _ = blocks.shape
    far = pl.BlockSpec(memory_space=pl.ANY)
    near = pl.BlockSpec(memory_space=pltpu.VMEM)
    rest = (rows - slots_of(rows)) * width
    most = -(-rows // BATCH) * BATCH
    rhs = given[0]
    out_shape = [jax.ShapeDtypeStruct(blocks.shape, BF), jax.ShapeDtypeStruct(rhs.shape, F32)]
    scratch = [
        pltpu.VMEM((2, n * height + rest, width), BF),
        pltpu.VMEM((most, width, 2 * width), BF),
        pltpu.VMEM((rows, cols, width, width), BF),
        pltpu.VMEM((2 * FLAG_ROWS, 128), jnp.int32),
        pltpu.SMEM((2 * FLAG_ROWS, 128), jnp.int32),
        pltpu.SMEM((2, rows), jnp.int32),
        pltpu.SMEM((rows + 1,), jnp.int32),
        pltpu.SemaphoreType.DMA((rows,)),
        pltpu.SemaphoreType.DMA((rows,)),
        pltpu.SemaphoreType.DMA,
    ]
    if last:
        scratch += [pltpu.VMEM(a.shape, a.dtype) for a in given]
        scratch += [pltpu.SemaphoreType.DMA((len(given) + 3,)), pltpu.SemaphoreType.DMA((n, 2))]
    else:
        out_shape.append(jax.ShapeDtypeStruct(extra[0].shape, F32))
    place = far if last else near
    arrays = (*given, *landed, *extra)
    return pl.pallas_call(
        functools.partial(update_kernel, n, height, nrows, ncols, sources, len(landed), last),
        in_specs=[pl.BlockSpec(memory_space=pltpu.SMEM), far] + [place] * len(arrays),
        out_specs=[far] + [near] * (len(out_shape) - 1),
        out_shape=out_shape,
        scratch_shapes=scratch,
        input_output_aliases={1 + len(arrays): 0} if last else {},
        compiler_params=pltpu.CompilerParams(vmem_limit_bytes=WIDE_VMEM if last else UPDATE_VMEM),
        cost_estimate=pl.CostEstimate(
            flops=2 * rows * (cols + 2) * width**3, bytes_accessed=2 * rows * (cols + 2) * width**2, transcendentals=0
        ),
    )(pattern, blocks, *arrays)


def on_device(blocks, pattern, pivot_inverse, right_sides):
    rows, cols, width, _ = blocks.shape
    dirs = right_sides.shape[1]
    nrows = lax.axis_size("rows")
    ncols = lax.axis_size("cols")
    groups = ncols // 2
    depth, own_from, other_depth, other_from, permutes = broadcast_plan(groups)
    n = max(d for d in range(2, MOST_CHUNKS + 1))
    height = chunk_height(rows, width, n)
    slots = slots_of(rows)
    pattern = pattern.T
    start, later, rest = pack(blocks, pattern, n, height)
    columns = [start] + [(later, k) for k in range(n - 1)]
    row = pack_row(blocks, pattern, right_sides)

    def among(members):
        return lambda row_device, col: functools.reduce(jnp.logical_or, [col // 2 == g for g in members])

    def down_rows(x):
        reach = 1
        while reach < nrows // 2:
            hops = [(2 * h + s, 2 * (h + reach) + s) for h in range(min(reach, nrows // 2 - reach)) for s in (0, 1)]
            moved = lax.ppermute(x, "rows", hops)
            bound = 2 * reach
            x = pick([(lambda r, c, b=bound: r < b, x), (lambda r, c, b=bound: r >= b, moved)])
            reach *= 2
        return x, lax.ppermute(x, "rows", [(r, r ^ 1) for r in range(nrows)])

    def across_rows(x):
        pairs, reach = nrows // 2, 1
        if pairs & (pairs - 1):
            flags = lax.pmax(x[width:].astype(F32), "rows").astype(BF)
            x = jnp.concatenate([x[:width], flags], 0)
            return down_rows(x)
        while reach < pairs:
            x = merge(2 * reach, x, lax.ppermute(x, "rows", [(r, r ^ (2 * reach)) for r in range(nrows)]))
            reach *= 2
        return x, lax.ppermute(x, "rows", [(r, r ^ 1) for r in range(nrows)])

    def places(k):
        own, cross = {}, {}
        for g in range(groups):
            key = ("here", k) if g == 0 else (own_from[g], k + depth[g] - 1)
            own.setdefault(key, []).append(g)
            cross.setdefault((other_from[g], k + other_depth[g]), []).append(g)
        return own, cross

    def array_at(key, columns, landed):
        return columns[key[1]] if key[0] == "here" else landed[key[1]][key[0]]

    def travel(columns, landed, step, after=()):
        count = len(columns)
        active = [g for g in range(groups) if 0 <= step - depth[g] < count]
        choices = []
        if 0 in active:
            choices.append((among([0]), columns[step]))
        for which in (0, 1):
            members = [g for g in active if g and own_from[g] == which]
            if members:
                choices.append((among(members), landed[step - 1][which]))
        payload = columns[0]
        if step:
            payload = pick(choices, after=[a for a in landed[-1] if a is not None] + list(after))
        pairs = [[p for p in permutes[which] if p[0] // 2 in active] for which in (0, 1)]
        return [lax.ppermute(payload, "cols", p) if p else None for p in pairs]

    deepest = max(other_depth.values())
    lag = max(max(depth.values()) - 1, deepest) + 1

    def corners():
        own, cross = ([(among(m), array_at(k, columns, landed)) for k, m in found.items()] for found in places(0))
        return across_rows(corner_of(own, cross, slots, width))

    def update_with(chunks, extra, last):
        arrays, sources = [], []
        for k in range(chunks):
            sources.append([])
            for which in places(k):
                found = []
                for key, members in which.items():
                    array, place = array_at(key, columns, landed), None
                    if isinstance(array, tuple):
                        array, place = array
                    found.append(((len(arrays), place), members))
                    arrays.append(array)
                sources[-1].append(found)
        given = (right_sides, upper, upper_one, sides, pivot_inverse)
        return update(n, height, nrows, ncols, sources, arrays, pattern, blocks, given, extra, last)

    mine, other = down_rows(row)
    landed = []
    for step in range(n + deepest):
        after = []
        if step == lag + 1:
            corner, other_corner = corners()
            after.append(corner)
        landed.append(travel(columns, landed, step, after))
    if n + deepest <= lag + 1:
        corner, other_corner = corners()
    upper, upper_one, sides, over = panel(dirs, cols, ncols, mine, other, corner, other_corner, pivot_inverse)
    out, forward, over = update_with(n - 1, (over,), False)

    def fetch_rest(rest):
        got = []
        for step in range(1 + deepest):
            got.append(travel([rest], got, step))
        own, cross = places(0)
        return tuple(pick([(among(m), array_at(k, [rest], got)) for k, m in found.items()]) for found in (own, cross))

    rest_own, rest_cross = lax.cond(over[0, 0] > 0.5, fetch_rest, lambda rest: (rest, rest), rest)
    return tuple(update_with(n, (rest_own, rest_cross, forward, out), True))


def solution(mesh):
    return jax.shard_map(
        on_device,
        mesh=mesh,
        in_specs=(P("rows", "cols", None, None), P("rows", "cols"), P(), P("rows", None, None)),
        out_specs=(P("rows", "cols", None, None), P("rows", None, None)),
        check_vma=False,
    )
```

```python
import functools

import jax
import jax.numpy as jnp
from jax import lax
from jax.experimental import pallas as pl
from jax.experimental.pallas import tpu as pltpu
from jax.sharding import PartitionSpec as P

BF = jnp.bfloat16
F32 = jnp.float32
FLAG_ROWS = 16
PIECE_ROWS = 32
MOST_CHUNKS = 3
BATCH = 4
WIDE_VMEM = 54 * 1024 * 1024
VMEM_LIMIT = 20 * 1024 * 1024
UPDATE_VMEM = 44 * 1024 * 1024


def broadcast_plan(groups):
    children = {g: [] for g in range(groups)}

    def hang(low, high, parent):
        if low < high:
            hub = (low + high) // 2
            children[parent].append(hub)
            hang(low, hub, hub)
            hang(hub + 1, high, hub)

    hang(1, groups, 0)
    depth = {0: 0}
    order = [0]
    for g in order:
        for child in children[g]:
            depth[child] = depth[g] + 1
            order.append(child)
    edges = [(g, child, 0) for g in order for child in children[g]]
    spare = {g: 2 - len(children[g]) for g in order}
    orphans = []
    for g in order:
        if spare[g]:
            edges.append((g, g, 1))
            spare[g] -= 1
        else:
            orphans.append(g)
    for g in orphans:
        helper = min((h for h in order if spare[h]), key=lambda h: (depth[h], -h))
        edges.append((helper, g, 1))
        spare[helper] -= 1
    colour = {}
    for start in range(len(edges)):
        if start in colour:
            continue
        colour[start] = 0
        stack = [start]
        while stack:
            e = stack.pop()
            for f in range(len(edges)):
                if f != e and f not in colour and (edges[f][0] == edges[e][0] or edges[f][1] == edges[e][1]):
                    colour[f] = 1 - colour[e]
                    stack.append(f)
    permutes = ([], [])
    own_from, other_from, other_depth = {0: 0}, {}, {}
    for e, (sender, receiver, cross) in enumerate(edges):
        for side in (0, 1):
            permutes[colour[e]].append((2 * sender + side, 2 * receiver + (side ^ cross)))
        if cross:
            other_from[receiver] = colour[e]
            other_depth[receiver] = depth[sender]
        else:
            own_from[receiver] = colour[e]
    return depth, own_from, other_depth, other_from, permutes


def dot(a, b):
    return jnp.dot(a, b, preferred_element_type=F32)


def dot_t(a, b):
    return lax.dot_general(a, b, (((1,), (1,)), ((), ())), preferred_element_type=F32)


def pieces_of(rows):
    n, w = rows.shape
    full = jnp.concatenate([rows, jnp.zeros((8 - n, w), F32)], 0) if n < 8 else rows
    high = full.astype(BF).astype(F32)
    middle = (full - high).astype(BF).astype(F32)
    low = full - high - middle
    return jnp.concatenate([high, middle, low, jnp.zeros((PIECE_ROWS - 24, w), F32)], 0).astype(BF)


def sum_pieces(x, n):
    return (x[0:8] + x[8:16] + x[16:24])[:n]


def slots_of(rows):
    return max(1, rows * 5 // 6)


def chunk_height(rows, width, n):
    return -(-(FLAG_ROWS + slots_of(rows) * width) // (16 * n)) * 16


def pack_kernel(n, height, pattern, column, first_out, later_out, rest_out, packed):
    rows, width = column.shape[0], column.shape[-1]
    slots = slots_of(rows)
    zero = jnp.zeros((), BF)
    lines = lax.broadcasted_iota(jnp.int32, (FLAG_ROWS, width), 0)
    flags = jnp.zeros((FLAG_ROWS, width), F32)
    place = jnp.int32(0)
    for i in range(rows):
        live = pattern[0, i] == 1
        occupied = live | (lax.axis_index("rows") < 2) if i == 0 else live
        start = jnp.where(place < slots, FLAG_ROWS + place * width, n * height + (place - slots) * width)

        @pl.when(occupied)
        def _(i=i, live=live, start=start):
            packed[pl.ds(pl.multiple_of(start, 16), width)] = jnp.where(live, column[i, 0], zero)

        flags = jnp.where((lines == i) & occupied, 1.0, flags)
        place = place + occupied.astype(jnp.int32)
    packed[0:FLAG_ROWS] = flags.astype(BF)
    first_out[...] = packed[0:height]
    for k in range(1, n):
        later_out[k - 1] = packed[k * height : (k + 1) * height]
    rest_out[...] = packed[n * height :]


def pack(blocks, pattern, n, height):
    rows, cols, width, _ = blocks.shape
    rest = (rows - slots_of(rows)) * width
    shapes = [(height, width), (n - 1, height, width), (rest, width)]
    near = pl.BlockSpec(memory_space=pltpu.VMEM)
    return pl.pallas_call(
        functools.partial(pack_kernel, n, height),
        grid=(1,),
        in_specs=[
            pl.BlockSpec(memory_space=pltpu.SMEM),
            pl.BlockSpec((rows, 1, width, width), lambda s: (0, 0, 0, 0)),
        ],
        out_specs=[near] * 3,
        out_shape=[jax.ShapeDtypeStruct(shape, BF) for shape in shapes],
        scratch_shapes=[pltpu.VMEM((n * height + rest, width), BF)],
        compiler_params=pltpu.CompilerParams(vmem_limit_bytes=WIDE_VMEM),
    )(pattern, blocks)


def row_kernel(pattern, row, rhs, out):
    cols, width = row.shape[1], row.shape[-1]
    lines = lax.broadcasted_iota(jnp.int32, (FLAG_ROWS, width), 0)
    flags = jnp.zeros((FLAG_ROWS, width), F32)
    for j in range(cols):
        live = pattern[j, 0] == 1
        out[j * width : (j + 1) * width] = jnp.where(live, row[0, j], jnp.zeros((), BF))
        flags = jnp.where((lines == j) & live, 1.0, flags)
    base = cols * width
    out[base : base + FLAG_ROWS] = flags.astype(BF)
    out[base + FLAG_ROWS : base + FLAG_ROWS + PIECE_ROWS] = pieces_of(rhs[0])


def pack_row(blocks, pattern, right_sides):
    rows, cols, width, _ = blocks.shape
    dirs = right_sides.shape[1]
    shape = (cols * width + FLAG_ROWS + PIECE_ROWS, width)
    return pl.pallas_call(
        row_kernel,
        grid=(1,),
        in_specs=[
            pl.BlockSpec(memory_space=pltpu.SMEM),
            pl.BlockSpec((1, cols, width, width), lambda s: (0, 0, 0, 0)),
            pl.BlockSpec((1, dirs, width), lambda s: (0, 0, 0)),
        ],
        out_specs=pl.BlockSpec(shape, lambda s: (0, 0)),
        out_shape=jax.ShapeDtypeStruct(shape, BF),
        compiler_params=pltpu.CompilerParams(vmem_limit_bytes=WIDE_VMEM),
    )(pattern, blocks, right_sides)


def pick_kernel(tests, places, start, height, *refs):
    sources, out = refs[: len(tests)], refs[-1]
    row_device, col = lax.axis_index("rows"), lax.axis_index("cols")
    for test, place, source in zip(tests, places, sources):

        @pl.when(test(row_device, col))
        def _(place=place, source=source):
            at = slice(start, start + height)
            out[...] = source[at] if place is None else source[place, at]


def pick(choices, start=0, height=None, after=()):
    tests, arrays, places = zip(*((t, *a) if isinstance(a, tuple) else (t, a, None) for t, a in choices))
    height = height or arrays[0].shape[-2]
    after = [a for a in after if all(a is not b for b in arrays)]
    near = pl.BlockSpec(memory_space=pltpu.VMEM)
    return pl.pallas_call(
        functools.partial(pick_kernel, tests, places, start, height),
        in_specs=[near] * len(arrays) + [pl.BlockSpec(memory_space=pl.ANY)] * len(after),
        out_specs=near,
        out_shape=jax.ShapeDtypeStruct((height, arrays[0].shape[-1]), BF),
        compiler_params=pltpu.CompilerParams(vmem_limit_bytes=VMEM_LIMIT),
    )(*arrays, *after)


def corner_kernel(own_tests, cross_tests, slots, *refs):
    sources, out, counts = refs[: len(own_tests) + len(cross_tests)], refs[-2], refs[-1]
    width = out.shape[0] - FLAG_ROWS
    row_device, col = lax.axis_index("rows"), lax.axis_index("cols")
    own_side = (col % 2 == 0) == (row_device % 2 == 1)
    counts[...] = jnp.zeros(counts.shape, F32)
    for k, (test, source) in enumerate(zip(own_tests + cross_tests, sources)):
        wanted = own_side if k < len(own_tests) else jnp.logical_not(own_side)

        @pl.when(test(row_device, col))
        def _(source=source, wanted=wanted):
            taken = jnp.sum(source[0:FLAG_ROWS].astype(F32), 0, keepdims=True)
            counts[...] = jnp.maximum(counts[...], taken)

            @pl.when(wanted)
            def _():
                out[0:width] = source[FLAG_ROWS : FLAG_ROWS + width]

    out[width:] = jnp.where(counts[0:FLAG_ROWS] > slots, 1.0, 0.0).astype(BF)


def corner_of(own, cross, slots, width):
    near = pl.BlockSpec(memory_space=pltpu.VMEM)
    own_tests, cross_tests = [t for t, _ in own], [t for t, _ in cross]
    return pl.pallas_call(
        functools.partial(corner_kernel, own_tests, cross_tests, slots),
        in_specs=[near] * len(own + cross),
        out_specs=near,
        out_shape=jax.ShapeDtypeStruct((width + FLAG_ROWS, width), BF),
        scratch_shapes=[pltpu.VMEM((FLAG_ROWS, width), F32)],
        compiler_params=pltpu.CompilerParams(vmem_limit_bytes=VMEM_LIMIT),
    )(*[a for _, a in own + cross])


def merge_kernel(bound, mine, moved, out):
    width = out.shape[0] - FLAG_ROWS
    keep = lax.axis_index("rows") < bound
    out[0:width] = jnp.where(keep, mine[0:width], moved[0:width])
    out[width:] = jnp.maximum(mine[width:].astype(F32), moved[width:].astype(F32)).astype(BF)


def merge(bound, mine, moved):
    near = pl.BlockSpec(memory_space=pltpu.VMEM)
    return pl.pallas_call(
        functools.partial(merge_kernel, bound),
        in_specs=[near] * 2,
        out_specs=near,
        out_shape=jax.ShapeDtypeStruct(mine.shape, BF),
        compiler_params=pltpu.CompilerParams(vmem_limit_bytes=VMEM_LIMIT),
    )(mine, moved)


def panel_kernel(dirs, ncols, mine, other, corner, other_corner, inverse, upper, upper_one, sides, over):
    width = inverse.shape[-1]
    cols = upper.shape[1] // width
    even = lax.axis_index("rows") % 2 == 0
    col = lax.axis_index("cols")

    def pick(lo, hi):
        a, b = mine[lo:hi], other[lo:hi]
        return jnp.where(even, a, b), jnp.where(even, b, a)

    zero = jnp.zeros((), BF)
    over[...] = jnp.maximum(corner[width:].astype(F32), other_corner[width:].astype(F32))[:, 0:128]
    upper_one[...] = jnp.where(even, corner[0:width], other_corner[0:width])
    lower_one = dot(jnp.where(even, other_corner[0:width], corner[0:width]), inverse[0]).astype(BF)
    base = cols * width
    flags = pick(base, base + FLAG_ROWS)[1].astype(F32)
    for j in range(cols):
        zeroth, first = pick(j * width, (j + 1) * width)
        zeroth = jnp.where(j * ncols + col > 0, zeroth, zero)
        fresh = (first.astype(F32) - dot(lower_one, zeroth)).astype(BF)
        keep = (flags[j : j + 1] > 0.5) & (j * ncols + col > 1)
        at = slice(j * width, (j + 1) * width)
        upper[0:width, at] = zeroth
        upper[width : 2 * width, at] = jnp.where(keep, fresh, zero)
    side_zero, side_one = pick(base + FLAG_ROWS, base + FLAG_ROWS + PIECE_ROWS)
    sides[0] = side_zero
    later = sum_pieces(side_one.astype(F32), dirs) - sum_pieces(dot_t(side_zero, lower_one), dirs)
    sides[1] = pieces_of(later)


def panel(dirs, cols, ncols, mine, other, corner, other_corner, inverse):
    width = inverse.shape[-1]
    return pl.pallas_call(
        functools.partial(panel_kernel, dirs, ncols),
        out_shape=[
            jax.ShapeDtypeStruct((2 * width, cols * width), BF),
            jax.ShapeDtypeStruct((width, width), BF),
            jax.ShapeDtypeStruct((2, PIECE_ROWS, width), BF),
            jax.ShapeDtypeStruct((FLAG_ROWS, 128), F32),
        ],
        compiler_params=pltpu.CompilerParams(vmem_limit_bytes=VMEM_LIMIT),
        cost_estimate=pl.CostEstimate(
            flops=2 * (cols + 2) * width**3, bytes_accessed=8 * cols * width**2, transcendentals=0
        ),
    )(mine, other, corner, other_corner, inverse)


def update_kernel(n, height, nrows, ncols, sources, n_refs, last, *refs):
    pattern, blocks = refs[:2]
    given, landed, extra = refs[2:7], refs[7 : 7 + n_refs], refs[7 + n_refs : 10 + n_refs]
    outs = refs[7 + n_refs + (4 if last else 1) :]
    out, forward = outs[:2]
    scratch = outs[2 if last else 3 :]
    columns, lower, work, flags_v, flags_s, slot_of, order, in_sems, out_sems, flag_sem = scratch[:10]
    row_device, col = lax.axis_index("rows"), lax.axis_index("cols")
    pair, side = col // 2, col % 2
    zero = jnp.zeros((), BF)
    rows, cols, width = work.shape[:3]
    slots = slots_of(rows)

    copies = []
    if last:
        near, given_sems, column_sems = scratch[10:15], scratch[15], scratch[16]
        rest_own, rest_cross, done = extra
        tail = slice(n * height, None)
        moves = list(zip(given, near)) + [(done, forward)]
        moves += [(rest_own, columns.at[side, tail]), (rest_cross, columns.at[1 - side, tail])]
        for m, (source, target) in enumerate(moves):
            copies.append(pltpu.make_async_copy(source, target, given_sems.at[m]))
            copies[-1].start()
    else:
        near = given
        outs[2][...] = extra[0][0:1, 0:1]
    rhs, upper, upper_one, sides, inverse = near

    for k, per_chunk in enumerate(sources):
        for which in (0, 1):
            for ref, pairs in per_chunk[which]:
                hit = functools.reduce(jnp.logical_or, [pair == g for g in pairs])

                @pl.when(hit)
                def _(source=landed[ref[0]], place=ref[1], which=which, k=k):
                    source = source if place is None else source.at[place]
                    at = slice(k * height, (k + 1) * height)
                    target = columns.at[side if which == 0 else 1 - side, at]
                    if last:
                        pltpu.make_async_copy(source, target, column_sems.at[k, which]).start()
                    else:
                        target[...] = source[...]

    if last:
        for copy in copies:
            copy.wait()
        for k in range(n):
            for which in (0, 1):
                at = slice(k * height, (k + 1) * height)
                target = columns.at[side if which == 0 else 1 - side, at]
                pltpu.make_async_copy(target, target, column_sems.at[k, which]).wait()

    for b in (0, 1):
        flags_v[b * FLAG_ROWS : (b + 1) * FLAG_ROWS] = columns[b, 0:FLAG_ROWS].astype(F32)[:, 0:128].astype(jnp.int32)
    copy = pltpu.make_async_copy(flags_v, flags_s, flag_sem)
    copy.start()
    copy.wait()

    early = ((n - 1) * height - FLAG_ROWS) // width
    zeroth = first = count = vacant = jnp.int32(0)
    for i in range(rows):
        occupied = flags_s[i, 0], flags_s[FLAG_ROWS + i, 0]
        slot_zeroth, slot_first = jnp.where(occupied[0] > 0, zeroth, -1), jnp.where(occupied[1] > 0, first, -1)
        slot_of[0, i] = slot_zeroth
        slot_of[1, i] = slot_first
        ready = (slot_zeroth < early) & (slot_first < early)
        mine = jnp.logical_not(ready) if last else ready
        empty = (slot_zeroth < 0) & (slot_first < 0)
        full = mine & jnp.logical_not(empty)
        order[jnp.where(empty, rows - 1 - vacant, count)] = i
        count = count + full.astype(jnp.int32)
        vacant = vacant + empty.astype(jnp.int32)
        zeroth, first = zeroth + occupied[0], first + occupied[1]

    def row_at(t):
        return order[jnp.minimum(t, count - 1)]

    def fetch(t):
        return pltpu.make_async_copy(blocks.at[order[t]], work.at[t], in_sems.at[t])

    def send(t):
        return pltpu.make_async_copy(work.at[t], out.at[order[t]], out_sems.at[t])

    @pl.loop(0, count)
    def _(t):
        fetch(t).start()

    if not last:

        @pl.loop(rows - vacant, rows)
        def _(t):
            fetch(t).start()

    if not last:
        forward[...] = rhs[...]

    def block_at(b, i):
        slot = slot_of[b, i]
        start = jnp.where(slot < slots, FLAG_ROWS + slot * width, n * height + (slot - slots) * width)
        start = jnp.where(slot < 0, 0, start)
        return jnp.where(slot >= 0, columns[b, pl.ds(pl.multiple_of(start, 16), width)], zero)

    @pl.loop(0, (count + BATCH - 1) // BATCH)
    def _(g):
        members = [row_at(g * BATCH + t) for t in range(BATCH)]
        globs = [i * nrows + row_device for i in members]
        parts = [slice(t * width, (t + 1) * width) for t in range(BATCH)]
        product = dot(jnp.concatenate([block_at(0, i) for i in members], 0), inverse[0])
        lower_zero = jnp.concatenate(
            [jnp.where(glob > 0, product[at], 0.0).astype(BF) for glob, at in zip(globs, parts)], 0
        )
        change = dot(lower_zero, upper_one[...])
        pivots = []
        for i, at in zip(members, parts):
            fresh = (block_at(1, i).astype(F32) - change[at]).astype(BF)
            pivots.append(jnp.where(slot_of[1, i] >= 0, fresh, zero))
        product = dot(jnp.concatenate(pivots, 0), inverse[1])
        for t, (glob, at) in enumerate(zip(globs, parts)):
            lower[g * BATCH + t, :, 0:width] = lower_zero[at]
            lower[g * BATCH + t, :, width : 2 * width] = jnp.where(glob > 1, product[at], 0.0).astype(BF)

    @pl.loop(0, count)
    def _(t):
        i = row_at(t)
        glob = i * nrows + row_device
        dirs = rhs.shape[1]
        fetch(t).wait()
        head = rhs[i] - sum_pieces(dot_t(sides[0], lower[t, :, 0:width]), dirs)
        forward[i] = head - sum_pieces(dot_t(sides[1], lower[t, :, width : 2 * width]), dirs)
        lower_zeroth = (col == 0) & (glob > 0)
        lower_first = (col == 1) & (glob > 1)
        for j in range(cols):
            change = dot(lower[t], upper[:, j * width : (j + 1) * width])
            fresh = (work[t, j].astype(F32) - change).astype(BF)
            fresh = jnp.where(pattern[j, i] == 1, fresh, zero)
            if j == 0:
                fresh = jnp.where(lower_zeroth, lower[t, :, 0:width], fresh)
                fresh = jnp.where(lower_first, lower[t, :, width : 2 * width], fresh)
            work[t, j] = fresh
        send(t).start()

    if not last:

        @pl.loop(rows - vacant, rows)
        def _(t):
            fetch(t).wait()
            for j in range(cols):
                work[t, j] = jnp.where(pattern[j, order[t]] == 1, work[t, j], zero)
            send(t).start()

        @pl.loop(rows - vacant, rows)
        def _(t):
            send(t).wait()

    @pl.loop(0, count)
    def _(t):
        send(t).wait()


def update(n, height, nrows, ncols, sources, landed, pattern, blocks, given, extra, last):
    rows, cols, width, _ = blocks.shape
    far = pl.BlockSpec(memory_space=pl.ANY)
    near = pl.BlockSpec(memory_space=pltpu.VMEM)
    rest = (rows - slots_of(rows)) * width
    most = -(-rows // BATCH) * BATCH
    rhs = given[0]
    out_shape = [jax.ShapeDtypeStruct(blocks.shape, BF), jax.ShapeDtypeStruct(rhs.shape, F32)]
    scratch = [
        pltpu.VMEM((2, n * height + rest, width), BF),
        pltpu.VMEM((most, width, 2 * width), BF),
        pltpu.VMEM((rows, cols, width, width), BF),
        pltpu.VMEM((2 * FLAG_ROWS, 128), jnp.int32),
        pltpu.SMEM((2 * FLAG_ROWS, 128), jnp.int32),
        pltpu.SMEM((2, rows), jnp.int32),
        pltpu.SMEM((rows + 1,), jnp.int32),
        pltpu.SemaphoreType.DMA((rows,)),
        pltpu.SemaphoreType.DMA((rows,)),
        pltpu.SemaphoreType.DMA,
    ]
    if last:
        scratch += [pltpu.VMEM(a.shape, a.dtype) for a in given]
        scratch += [pltpu.SemaphoreType.DMA((len(given) + 3,)), pltpu.SemaphoreType.DMA((n, 2))]
    else:
        out_shape.append(jax.ShapeDtypeStruct((1, 1), F32))
    place = far if last else near
    arrays = (*given, *landed, *extra)
    return pl.pallas_call(
        functools.partial(update_kernel, n, height, nrows, ncols, sources, len(landed), last),
        in_specs=[pl.BlockSpec(memory_space=pltpu.SMEM), far] + [place] * len(arrays),
        out_specs=[far] + [near] * (len(out_shape) - 1),
        out_shape=out_shape,
        scratch_shapes=scratch,
        input_output_aliases={1 + len(arrays): 0} if last else {},
        compiler_params=pltpu.CompilerParams(vmem_limit_bytes=WIDE_VMEM if last else UPDATE_VMEM),
        cost_estimate=pl.CostEstimate(
            flops=2 * rows * (cols + 2) * width**3, bytes_accessed=2 * rows * (cols + 2) * width**2, transcendentals=0
        ),
    )(pattern, blocks, *arrays)


def on_device(blocks, pattern, pivot_inverse, right_sides):
    rows, cols, width, _ = blocks.shape
    dirs = right_sides.shape[1]
    nrows = lax.axis_size("rows")
    ncols = lax.axis_size("cols")
    groups = ncols // 2
    depth, own_from, other_depth, other_from, permutes = broadcast_plan(groups)
    n = max(d for d in range(2, MOST_CHUNKS + 1))
    height = chunk_height(rows, width, n)
    slots = slots_of(rows)
    pattern = pattern.T
    start, later, rest = pack(blocks, pattern, n, height)
    columns = [start] + [(later, k) for k in range(n - 1)]
    row = pack_row(blocks, pattern, right_sides)

    def among(members):
        return lambda row_device, col: functools.reduce(jnp.logical_or, [col // 2 == g for g in members])

    def down_rows(x):
        reach = 1
        while reach < nrows // 2:
            hops = [(2 * h + s, 2 * (h + reach) + s) for h in range(min(reach, nrows // 2 - reach)) for s in (0, 1)]
            moved = lax.ppermute(x, "rows", hops)
            bound = 2 * reach
            x = pick([(lambda r, c, b=bound: r < b, x), (lambda r, c, b=bound: r >= b, moved)])
            reach *= 2
        return x, lax.ppermute(x, "rows", [(r, r ^ 1) for r in range(nrows)])

    def across_rows(x):
        pairs, reach = nrows // 2, 1
        if pairs & (pairs - 1):
            flags = lax.pmax(x[width:].astype(F32), "rows").astype(BF)
            x = jnp.concatenate([x[:width], flags], 0)
            return down_rows(x)
        while reach < pairs:
            x = merge(2 * reach, x, lax.ppermute(x, "rows", [(r, r ^ (2 * reach)) for r in range(nrows)]))
            reach *= 2
        return x, lax.ppermute(x, "rows", [(r, r ^ 1) for r in range(nrows)])

    def places(k):
        own, cross = {}, {}
        for g in range(groups):
            key = ("here", k) if g == 0 else (own_from[g], k + depth[g] - 1)
            own.setdefault(key, []).append(g)
            cross.setdefault((other_from[g], k + other_depth[g]), []).append(g)
        return own, cross

    def array_at(key, columns, landed):
        return columns[key[1]] if key[0] == "here" else landed[key[1]][key[0]]

    def travel(columns, landed, step, after=()):
        count = len(columns)
        active = [g for g in range(groups) if 0 <= step - depth[g] < count]
        choices = []
        if 0 in active:
            choices.append((among([0]), columns[step]))
        for which in (0, 1):
            members = [g for g in active if g and own_from[g] == which]
            if members:
                choices.append((among(members), landed[step - 1][which]))
        payload = columns[0]
        if step:
            payload = pick(choices, after=[a for a in landed[-1] if a is not None] + list(after))
        pairs = [[p for p in permutes[which] if p[0] // 2 in active] for which in (0, 1)]
        return [lax.ppermute(payload, "cols", p) if p else None for p in pairs]

    deepest = max(other_depth.values())
    lag = max(max(depth.values()) - 1, deepest) + 1

    def corners():
        own, cross = ([(among(m), array_at(k, columns, landed)) for k, m in found.items()] for found in places(0))
        return across_rows(corner_of(own, cross, slots, width))

    def update_with(chunks, extra, last):
        arrays, sources = [], []
        for k in range(chunks):
            sources.append([])
            for which in places(k):
                found = []
                for key, members in which.items():
                    array, place = array_at(key, columns, landed), None
                    if isinstance(array, tuple):
                        array, place = array
                    found.append(((len(arrays), place), members))
                    arrays.append(array)
                sources[-1].append(found)
        given = (right_sides, upper, upper_one, sides, pivot_inverse)
        return update(n, height, nrows, ncols, sources, arrays, pattern, blocks, given, extra, last)

    mine, other = down_rows(row)
    landed = []
    for step in range(n + deepest):
        after = []
        if step == lag + 1:
            corner, other_corner = corners()
            after.append(corner)
        landed.append(travel(columns, landed, step, after))
    if n + deepest <= lag + 1:
        corner, other_corner = corners()
    upper, upper_one, sides, over = panel(dirs, cols, ncols, mine, other, corner, other_corner, pivot_inverse)
    out, forward, over = update_with(n - 1, (over,), False)

    def fetch_rest(rest):
        got = []
        for step in range(1 + deepest):
            got.append(travel([rest], got, step))
        own, cross = places(0)
        return tuple(pick([(among(m), array_at(k, [rest], got)) for k, m in found.items()]) for found in (own, cross))

    rest_own, rest_cross = lax.cond(over[0, 0] > 0.5, fetch_rest, lambda rest: (rest, rest), rest)
    return tuple(update_with(n, (rest_own, rest_cross, forward, out), True))


def solution(mesh):
    return jax.shard_map(
        on_device,
        mesh=mesh,
        in_specs=(P("rows", "cols", None, None), P("rows", "cols"), P(), P("rows", None, None)),
        out_specs=(P("rows", "cols", None, None), P("rows", None, None)),
        check_vma=False,
    )
```

```python
import functools

import jax
import jax.numpy as jnp
from jax import lax
from jax.experimental import pallas as pl
from jax.experimental.pallas import tpu as pltpu
from jax.sharding import PartitionSpec as P

BF = jnp.bfloat16
F32 = jnp.float32
FLAG_ROWS = 16
PIECE_ROWS = 32
MOST_CHUNKS = 3
BATCH = 4
WIDE_VMEM = 54 * 1024 * 1024
VMEM_LIMIT = 20 * 1024 * 1024
UPDATE_VMEM = 44 * 1024 * 1024


def broadcast_plan(groups):
    children = {g: [] for g in range(groups)}

    def hang(low, high, parent):
        if low < high:
            hub = (low + high) // 2
            children[parent].append(hub)
            hang(low, hub, hub)
            hang(hub + 1, high, hub)

    hang(1, groups, 0)
    depth = {0: 0}
    order = [0]
    for g in order:
        for child in children[g]:
            depth[child] = depth[g] + 1
            order.append(child)
    edges = [(g, child, 0) for g in order for child in children[g]]
    spare = {g: 2 - len(children[g]) for g in order}
    orphans = []
    for g in order:
        if spare[g]:
            edges.append((g, g, 1))
            spare[g] -= 1
        else:
            orphans.append(g)
    for g in orphans:
        helper = min((h for h in order if spare[h]), key=lambda h: (depth[h], -h))
        edges.append((helper, g, 1))
        spare[helper] -= 1
    colour = {}
    for start in range(len(edges)):
        if start in colour:
            continue
        colour[start] = 0
        stack = [start]
        while stack:
            e = stack.pop()
            for f in range(len(edges)):
                if f != e and f not in colour and (edges[f][0] == edges[e][0] or edges[f][1] == edges[e][1]):
                    colour[f] = 1 - colour[e]
                    stack.append(f)
    permutes = ([], [])
    own_from, other_from, other_depth = {0: 0}, {}, {}
    for e, (sender, receiver, cross) in enumerate(edges):
        for side in (0, 1):
            permutes[colour[e]].append((2 * sender + side, 2 * receiver + (side ^ cross)))
        if cross:
            other_from[receiver] = colour[e]
            other_depth[receiver] = depth[sender]
        else:
            own_from[receiver] = colour[e]
    return depth, own_from, other_depth, other_from, permutes


def dot(a, b):
    return jnp.dot(a, b, preferred_element_type=F32)


def dot_t(a, b):
    return lax.dot_general(a, b, (((1,), (1,)), ((), ())), preferred_element_type=F32)


def pieces_of(rows):
    n, w = rows.shape
    full = jnp.concatenate([rows, jnp.zeros((8 - n, w), F32)], 0) if n < 8 else rows
    high = full.astype(BF).astype(F32)
    middle = (full - high).astype(BF).astype(F32)
    low = full - high - middle
    return jnp.concatenate([high, middle, low, jnp.zeros((PIECE_ROWS - 24, w), F32)], 0).astype(BF)


def sum_pieces(x, n):
    return (x[0:8] + x[8:16] + x[16:24])[:n]


def slots_of(rows):
    return max(1, rows * 3 // 4)


def chunk_height(rows, width, n):
    return -(-(FLAG_ROWS + slots_of(rows) * width) // (16 * n)) * 16


def pack_kernel(n, height, pattern, column, first_out, later_out, rest_out, packed):
    rows, width = column.shape[0], column.shape[-1]
    slots = slots_of(rows)
    zero = jnp.zeros((), BF)
    lines = lax.broadcasted_iota(jnp.int32, (FLAG_ROWS, width), 0)
    flags = jnp.zeros((FLAG_ROWS, width), F32)
    place = jnp.int32(0)
    for i in range(rows):
        live = pattern[0, i] == 1
        occupied = live | (lax.axis_index("rows") < 2) if i == 0 else live
        start = jnp.where(place < slots, FLAG_ROWS + place * width, n * height + (place - slots) * width)

        @pl.when(occupied)
        def _(i=i, live=live, start=start):
            packed[pl.ds(pl.multiple_of(start, 16), width)] = jnp.where(live, column[i, 0], zero)

        flags = jnp.where((lines == i) & occupied, 1.0, flags)
        place = place + occupied.astype(jnp.int32)
    packed[0:FLAG_ROWS] = flags.astype(BF)
    first_out[...] = packed[0:height]
    for k in range(1, n):
        later_out[k - 1] = packed[k * height : (k + 1) * height]
    rest_out[...] = packed[n * height :]


def pack(blocks, pattern, n, height):
    rows, cols, width, _ = blocks.shape
    rest = (rows - slots_of(rows)) * width
    shapes = [(height, width), (n - 1, height, width), (rest, width)]
    near = pl.BlockSpec(memory_space=pltpu.VMEM)
    return pl.pallas_call(
        functools.partial(pack_kernel, n, height),
        grid=(1,),
        in_specs=[
            pl.BlockSpec(memory_space=pltpu.SMEM),
            pl.BlockSpec((rows, 1, width, width), lambda s: (0, 0, 0, 0)),
        ],
        out_specs=[near] * 3,
        out_shape=[jax.ShapeDtypeStruct(shape, BF) for shape in shapes],
        scratch_shapes=[pltpu.VMEM((n * height + rest, width), BF)],
        compiler_params=pltpu.CompilerParams(vmem_limit_bytes=WIDE_VMEM),
    )(pattern, blocks)


def row_kernel(pattern, row, rhs, out):
    cols, width = row.shape[1], row.shape[-1]
    lines = lax.broadcasted_iota(jnp.int32, (FLAG_ROWS, width), 0)
    flags = jnp.zeros((FLAG_ROWS, width), F32)
    for j in range(cols):
        live = pattern[j, 0] == 1
        out[j * width : (j + 1) * width] = jnp.where(live, row[0, j], jnp.zeros((), BF))
        flags = jnp.where((lines == j) & live, 1.0, flags)
    base = cols * width
    out[base : base + FLAG_ROWS] = flags.astype(BF)
    out[base + FLAG_ROWS : base + FLAG_ROWS + PIECE_ROWS] = pieces_of(rhs[0])


def pack_row(blocks, pattern, right_sides):
    rows, cols, width, _ = blocks.shape
    dirs = right_sides.shape[1]
    shape = (cols * width + FLAG_ROWS + PIECE_ROWS, width)
    return pl.pallas_call(
        row_kernel,
        grid=(1,),
        in_specs=[
            pl.BlockSpec(memory_space=pltpu.SMEM),
            pl.BlockSpec((1, cols, width, width), lambda s: (0, 0, 0, 0)),
            pl.BlockSpec((1, dirs, width), lambda s: (0, 0, 0)),
        ],
        out_specs=pl.BlockSpec(shape, lambda s: (0, 0)),
        out_shape=jax.ShapeDtypeStruct(shape, BF),
        compiler_params=pltpu.CompilerParams(vmem_limit_bytes=WIDE_VMEM),
    )(pattern, blocks, right_sides)


def pick_kernel(tests, places, start, height, *refs):
    sources, out = refs[: len(tests)], refs[-1]
    row_device, col = lax.axis_index("rows"), lax.axis_index("cols")
    for test, place, source in zip(tests, places, sources):

        @pl.when(test(row_device, col))
        def _(place=place, source=source):
            at = slice(start, start + height)
            out[...] = source[at] if place is None else source[place, at]


def pick(choices, start=0, height=None, after=()):
    tests, arrays, places = zip(*((t, *a) if isinstance(a, tuple) else (t, a, None) for t, a in choices))
    height = height or arrays[0].shape[-2]
    after = [a for a in after if all(a is not b for b in arrays)]
    near = pl.BlockSpec(memory_space=pltpu.VMEM)
    return pl.pallas_call(
        functools.partial(pick_kernel, tests, places, start, height),
        in_specs=[near] * len(arrays) + [pl.BlockSpec(memory_space=pl.ANY)] * len(after),
        out_specs=near,
        out_shape=jax.ShapeDtypeStruct((height, arrays[0].shape[-1]), BF),
        compiler_params=pltpu.CompilerParams(vmem_limit_bytes=VMEM_LIMIT),
    )(*arrays, *after)


def corner_kernel(own_tests, cross_tests, slots, *refs):
    sources, out, counts = refs[: len(own_tests) + len(cross_tests)], refs[-2], refs[-1]
    width = out.shape[0] - FLAG_ROWS
    row_device, col = lax.axis_index("rows"), lax.axis_index("cols")
    own_side = (col % 2 == 0) == (row_device % 2 == 1)
    counts[...] = jnp.zeros(counts.shape, F32)
    for k, (test, source) in enumerate(zip(own_tests + cross_tests, sources)):
        wanted = own_side if k < len(own_tests) else jnp.logical_not(own_side)

        @pl.when(test(row_device, col))
        def _(source=source, wanted=wanted):
            taken = jnp.sum(source[0:FLAG_ROWS].astype(F32), 0, keepdims=True)
            counts[...] = jnp.maximum(counts[...], taken)

            @pl.when(wanted)
            def _():
                out[0:width] = source[FLAG_ROWS : FLAG_ROWS + width]

    out[width:] = jnp.where(counts[0:FLAG_ROWS] > slots, 1.0, 0.0).astype(BF)


def corner_of(own, cross, slots, width):
    near = pl.BlockSpec(memory_space=pltpu.VMEM)
    own_tests, cross_tests = [t for t, _ in own], [t for t, _ in cross]
    return pl.pallas_call(
        functools.partial(corner_kernel, own_tests, cross_tests, slots),
        in_specs=[near] * len(own + cross),
        out_specs=near,
        out_shape=jax.ShapeDtypeStruct((width + FLAG_ROWS, width), BF),
        scratch_shapes=[pltpu.VMEM((FLAG_ROWS, width), F32)],
        compiler_params=pltpu.CompilerParams(vmem_limit_bytes=VMEM_LIMIT),
    )(*[a for _, a in own + cross])


def merge_kernel(bound, mine, moved, out):
    width = out.shape[0] - FLAG_ROWS
    keep = lax.axis_index("rows") < bound
    out[0:width] = jnp.where(keep, mine[0:width], moved[0:width])
    out[width:] = jnp.maximum(mine[width:].astype(F32), moved[width:].astype(F32)).astype(BF)


def merge(bound, mine, moved):
    near = pl.BlockSpec(memory_space=pltpu.VMEM)
    return pl.pallas_call(
        functools.partial(merge_kernel, bound),
        in_specs=[near] * 2,
        out_specs=near,
        out_shape=jax.ShapeDtypeStruct(mine.shape, BF),
        compiler_params=pltpu.CompilerParams(vmem_limit_bytes=VMEM_LIMIT),
    )(mine, moved)


def panel_kernel(dirs, ncols, mine, other, corner, other_corner, inverse, upper, upper_one, sides, over):
    width = inverse.shape[-1]
    cols = upper.shape[1] // width
    even = lax.axis_index("rows") % 2 == 0
    col = lax.axis_index("cols")

    def pick(lo, hi):
        a, b = mine[lo:hi], other[lo:hi]
        return jnp.where(even, a, b), jnp.where(even, b, a)

    zero = jnp.zeros((), BF)
    over[...] = jnp.maximum(corner[width:].astype(F32), other_corner[width:].astype(F32))[:, 0:128]
    upper_one[...] = jnp.where(even, corner[0:width], other_corner[0:width])
    lower_one = dot(jnp.where(even, other_corner[0:width], corner[0:width]), inverse[0]).astype(BF)
    base = cols * width
    flags = pick(base, base + FLAG_ROWS)[1].astype(F32)
    for j in range(cols):
        zeroth, first = pick(j * width, (j + 1) * width)
        zeroth = jnp.where(j * ncols + col > 0, zeroth, zero)
        fresh = (first.astype(F32) - dot(lower_one, zeroth)).astype(BF)
        keep = (flags[j : j + 1] > 0.5) & (j * ncols + col > 1)
        at = slice(j * width, (j + 1) * width)
        upper[0:width, at] = zeroth
        upper[width : 2 * width, at] = jnp.where(keep, fresh, zero)
    side_zero, side_one = pick(base + FLAG_ROWS, base + FLAG_ROWS + PIECE_ROWS)
    sides[0] = side_zero
    later = sum_pieces(side_one.astype(F32), dirs) - sum_pieces(dot_t(side_zero, lower_one), dirs)
    sides[1] = pieces_of(later)


def panel(dirs, cols, ncols, mine, other, corner, other_corner, inverse):
    width = inverse.shape[-1]
    return pl.pallas_call(
        functools.partial(panel_kernel, dirs, ncols),
        out_shape=[
            jax.ShapeDtypeStruct((2 * width, cols * width), BF),
            jax.ShapeDtypeStruct((width, width), BF),
            jax.ShapeDtypeStruct((2, PIECE_ROWS, width), BF),
            jax.ShapeDtypeStruct((FLAG_ROWS, 128), F32),
        ],
        compiler_params=pltpu.CompilerParams(vmem_limit_bytes=VMEM_LIMIT),
        cost_estimate=pl.CostEstimate(
            flops=2 * (cols + 2) * width**3, bytes_accessed=8 * cols * width**2, transcendentals=0
        ),
    )(mine, other, corner, other_corner, inverse)


def update_kernel(n, height, nrows, ncols, sources, n_refs, last, *refs):
    pattern, blocks = refs[:2]
    given, landed, extra = refs[2:7], refs[7 : 7 + n_refs], refs[7 + n_refs : 10 + n_refs]
    outs = refs[7 + n_refs + (4 if last else 1) :]
    out, forward = outs[:2]
    scratch = outs[2 if last else 3 :]
    columns, lower, work, flags_v, flags_s, slot_of, order, in_sems, out_sems, flag_sem = scratch[:10]
    row_device, col = lax.axis_index("rows"), lax.axis_index("cols")
    pair, side = col // 2, col % 2
    zero = jnp.zeros((), BF)
    rows, cols, width = work.shape[:3]
    slots = slots_of(rows)

    copies = []
    if last:
        near, given_sems, column_sems = scratch[10:15], scratch[15], scratch[16]
        rest_own, rest_cross, done = extra
        tail = slice(n * height, None)
        moves = list(zip(given, near)) + [(done, forward)]
        moves += [(rest_own, columns.at[side, tail]), (rest_cross, columns.at[1 - side, tail])]
        for m, (source, target) in enumerate(moves):
            copies.append(pltpu.make_async_copy(source, target, given_sems.at[m]))
            copies[-1].start()
    else:
        near = given
        outs[2][...] = extra[0][0:1, 0:1]
    rhs, upper, upper_one, sides, inverse = near

    for k, per_chunk in enumerate(sources):
        for which in (0, 1):
            for ref, pairs in per_chunk[which]:
                hit = functools.reduce(jnp.logical_or, [pair == g for g in pairs])

                @pl.when(hit)
                def _(source=landed[ref[0]], place=ref[1], which=which, k=k):
                    source = source if place is None else source.at[place]
                    at = slice(k * height, (k + 1) * height)
                    target = columns.at[side if which == 0 else 1 - side, at]
                    if last:
                        pltpu.make_async_copy(source, target, column_sems.at[k, which]).start()
                    else:
                        target[...] = source[...]

    if last:
        for copy in copies:
            copy.wait()
        for k in range(n):
            for which in (0, 1):
                at = slice(k * height, (k + 1) * height)
                target = columns.at[side if which == 0 else 1 - side, at]
                pltpu.make_async_copy(target, target, column_sems.at[k, which]).wait()

    for b in (0, 1):
        flags_v[b * FLAG_ROWS : (b + 1) * FLAG_ROWS] = columns[b, 0:FLAG_ROWS].astype(F32)[:, 0:128].astype(jnp.int32)
    copy = pltpu.make_async_copy(flags_v, flags_s, flag_sem)
    copy.start()
    copy.wait()

    early = ((n - 1) * height - FLAG_ROWS) // width
    zeroth = first = count = vacant = jnp.int32(0)
    for i in range(rows):
        occupied = flags_s[i, 0], flags_s[FLAG_ROWS + i, 0]
        slot_zeroth, slot_first = jnp.where(occupied[0] > 0, zeroth, -1), jnp.where(occupied[1] > 0, first, -1)
        slot_of[0, i] = slot_zeroth
        slot_of[1, i] = slot_first
        ready = (slot_zeroth < early) & (slot_first < early)
        mine = jnp.logical_not(ready) if last else ready
        empty = (slot_zeroth < 0) & (slot_first < 0)
        full = mine & jnp.logical_not(empty)
        order[jnp.where(empty, rows - 1 - vacant, count)] = i
        count = count + full.astype(jnp.int32)
        vacant = vacant + empty.astype(jnp.int32)
        zeroth, first = zeroth + occupied[0], first + occupied[1]

    def row_at(t):
        return order[jnp.minimum(t, count - 1)]

    def fetch(t):
        return pltpu.make_async_copy(blocks.at[order[t]], work.at[t], in_sems.at[t])

    def send(t):
        return pltpu.make_async_copy(work.at[t], out.at[order[t]], out_sems.at[t])

    @pl.loop(0, count)
    def _(t):
        fetch(t).start()

    if not last:

        @pl.loop(rows - vacant, rows)
        def _(t):
            fetch(t).start()

    if not last:
        forward[...] = rhs[...]

    def block_at(b, i):
        slot = slot_of[b, i]
        start = jnp.where(slot < slots, FLAG_ROWS + slot * width, n * height + (slot - slots) * width)
        start = jnp.where(slot < 0, 0, start)
        return jnp.where(slot >= 0, columns[b, pl.ds(pl.multiple_of(start, 16), width)], zero)

    @pl.loop(0, (count + BATCH - 1) // BATCH)
    def _(g):
        members = [row_at(g * BATCH + t) for t in range(BATCH)]
        globs = [i * nrows + row_device for i in members]
        parts = [slice(t * width, (t + 1) * width) for t in range(BATCH)]
        product = dot(jnp.concatenate([block_at(0, i) for i in members], 0), inverse[0])
        lower_zero = jnp.concatenate(
            [jnp.where(glob > 0, product[at], 0.0).astype(BF) for glob, at in zip(globs, parts)], 0
        )
        change = dot(lower_zero, upper_one[...])
        pivots = []
        for i, at in zip(members, parts):
            fresh = (block_at(1, i).astype(F32) - change[at]).astype(BF)
            pivots.append(jnp.where(slot_of[1, i] >= 0, fresh, zero))
        product = dot(jnp.concatenate(pivots, 0), inverse[1])
        for t, (glob, at) in enumerate(zip(globs, parts)):
            lower[g * BATCH + t, :, 0:width] = lower_zero[at]
            lower[g * BATCH + t, :, width : 2 * width] = jnp.where(glob > 1, product[at], 0.0).astype(BF)

    @pl.loop(0, count)
    def _(t):
        i = row_at(t)
        glob = i * nrows + row_device
        dirs = rhs.shape[1]
        fetch(t).wait()
        head = rhs[i] - sum_pieces(dot_t(sides[0], lower[t, :, 0:width]), dirs)
        forward[i] = head - sum_pieces(dot_t(sides[1], lower[t, :, width : 2 * width]), dirs)
        lower_zeroth = (col == 0) & (glob > 0)
        lower_first = (col == 1) & (glob > 1)
        for j in range(cols):
            change = dot(lower[t], upper[:, j * width : (j + 1) * width])
            fresh = (work[t, j].astype(F32) - change).astype(BF)
            fresh = jnp.where(pattern[j, i] == 1, fresh, zero)
            if j == 0:
                fresh = jnp.where(lower_zeroth, lower[t, :, 0:width], fresh)
                fresh = jnp.where(lower_first, lower[t, :, width : 2 * width], fresh)
            work[t, j] = fresh
        send(t).start()

    if not last:

        @pl.loop(rows - vacant, rows)
        def _(t):
            fetch(t).wait()
            for j in range(cols):
                work[t, j] = jnp.where(pattern[j, order[t]] == 1, work[t, j], zero)
            send(t).start()

        @pl.loop(rows - vacant, rows)
        def _(t):
            send(t).wait()

    @pl.loop(0, count)
    def _(t):
        send(t).wait()


def update(n, height, nrows, ncols, sources, landed, pattern, blocks, given, extra, last):
    rows, cols, width, _ = blocks.shape
    far = pl.BlockSpec(memory_space=pl.ANY)
    near = pl.BlockSpec(memory_space=pltpu.VMEM)
    rest = (rows - slots_of(rows)) * width
    most = -(-rows // BATCH) * BATCH
    rhs = given[0]
    out_shape = [jax.ShapeDtypeStruct(blocks.shape, BF), jax.ShapeDtypeStruct(rhs.shape, F32)]
    scratch = [
        pltpu.VMEM((2, n * height + rest, width), BF),
        pltpu.VMEM((most, width, 2 * width), BF),
        pltpu.VMEM((rows, cols, width, width), BF),
        pltpu.VMEM((2 * FLAG_ROWS, 128), jnp.int32),
        pltpu.SMEM((2 * FLAG_ROWS, 128), jnp.int32),
        pltpu.SMEM((2, rows), jnp.int32),
        pltpu.SMEM((rows + 1,), jnp.int32),
        pltpu.SemaphoreType.DMA((rows,)),
        pltpu.SemaphoreType.DMA((rows,)),
        pltpu.SemaphoreType.DMA,
    ]
    if last:
        scratch += [pltpu.VMEM(a.shape, a.dtype) for a in given]
        scratch += [pltpu.SemaphoreType.DMA((len(given) + 3,)), pltpu.SemaphoreType.DMA((n, 2))]
    else:
        out_shape.append(jax.ShapeDtypeStruct((1, 1), F32))
    place = far if last else near
    arrays = (*given, *landed, *extra)
    return pl.pallas_call(
        functools.partial(update_kernel, n, height, nrows, ncols, sources, len(landed), last),
        in_specs=[pl.BlockSpec(memory_space=pltpu.SMEM), far] + [place] * len(arrays),
        out_specs=[far] + [near] * (len(out_shape) - 1),
        out_shape=out_shape,
        scratch_shapes=scratch,
        input_output_aliases={1 + len(arrays): 0} if last else {},
        compiler_params=pltpu.CompilerParams(vmem_limit_bytes=WIDE_VMEM if last else UPDATE_VMEM),
        cost_estimate=pl.CostEstimate(
            flops=2 * rows * (cols + 2) * width**3, bytes_accessed=2 * rows * (cols + 2) * width**2, transcendentals=0
        ),
    )(pattern, blocks, *arrays)


def on_device(blocks, pattern, pivot_inverse, right_sides):
    rows, cols, width, _ = blocks.shape
    dirs = right_sides.shape[1]
    nrows = lax.axis_size("rows")
    ncols = lax.axis_size("cols")
    groups = ncols // 2
    depth, own_from, other_depth, other_from, permutes = broadcast_plan(groups)
    n = max(d for d in range(2, MOST_CHUNKS + 1))
    height = chunk_height(rows, width, n)
    slots = slots_of(rows)
    pattern = pattern.T
    start, later, rest = pack(blocks, pattern, n, height)
    columns = [start] + [(later, k) for k in range(n - 1)]
    row = pack_row(blocks, pattern, right_sides)

    def among(members):
        return lambda row_device, col: functools.reduce(jnp.logical_or, [col // 2 == g for g in members])

    def down_rows(x):
        reach = 1
        while reach < nrows // 2:
            hops = [(2 * h + s, 2 * (h + reach) + s) for h in range(min(reach, nrows // 2 - reach)) for s in (0, 1)]
            moved = lax.ppermute(x, "rows", hops)
            bound = 2 * reach
            x = pick([(lambda r, c, b=bound: r < b, x), (lambda r, c, b=bound: r >= b, moved)])
            reach *= 2
        return x, lax.ppermute(x, "rows", [(r, r ^ 1) for r in range(nrows)])

    def across_rows(x):
        pairs, reach = nrows // 2, 1
        if pairs & (pairs - 1):
            flags = lax.pmax(x[width:].astype(F32), "rows").astype(BF)
            x = jnp.concatenate([x[:width], flags], 0)
            return down_rows(x)
        while reach < pairs:
            x = merge(2 * reach, x, lax.ppermute(x, "rows", [(r, r ^ (2 * reach)) for r in range(nrows)]))
            reach *= 2
        return x, lax.ppermute(x, "rows", [(r, r ^ 1) for r in range(nrows)])

    def places(k):
        own, cross = {}, {}
        for g in range(groups):
            key = ("here", k) if g == 0 else (own_from[g], k + depth[g] - 1)
            own.setdefault(key, []).append(g)
            cross.setdefault((other_from[g], k + other_depth[g]), []).append(g)
        return own, cross

    def array_at(key, columns, landed):
        return columns[key[1]] if key[0] == "here" else landed[key[1]][key[0]]

    def travel(columns, landed, step, after=()):
        count = len(columns)
        active = [g for g in range(groups) if 0 <= step - depth[g] < count]
        choices = []
        if 0 in active:
            choices.append((among([0]), columns[step]))
        for which in (0, 1):
            members = [g for g in active if g and own_from[g] == which]
            if members:
                choices.append((among(members), landed[step - 1][which]))
        payload = columns[0]
        if step:
            payload = pick(choices, after=[a for a in landed[-1] if a is not None] + list(after))
        pairs = [[p for p in permutes[which] if p[0] // 2 in active] for which in (0, 1)]
        return [lax.ppermute(payload, "cols", p) if p else None for p in pairs]

    deepest = max(other_depth.values())
    lag = max(max(depth.values()) - 1, deepest) + 1

    def corners():
        own, cross = ([(among(m), array_at(k, columns, landed)) for k, m in found.items()] for found in places(0))
        return across_rows(corner_of(own, cross, slots, width))

    def update_with(chunks, extra, last):
        arrays, sources = [], []
        for k in range(chunks):
            sources.append([])
            for which in places(k):
                found = []
                for key, members in which.items():
                    array, place = array_at(key, columns, landed), None
                    if isinstance(array, tuple):
                        array, place = array
                    found.append(((len(arrays), place), members))
                    arrays.append(array)
                sources[-1].append(found)
        given = (right_sides, upper, upper_one, sides, pivot_inverse)
        return update(n, height, nrows, ncols, sources, arrays, pattern, blocks, given, extra, last)

    mine, other = down_rows(row)
    landed = []
    for step in range(n + deepest):
        after = []
        if step == lag + 1:
            corner, other_corner = corners()
            after.append(corner)
        landed.append(travel(columns, landed, step, after))
    if n + deepest <= lag + 1:
        corner, other_corner = corners()
    upper, upper_one, sides, over = panel(dirs, cols, ncols, mine, other, corner, other_corner, pivot_inverse)
    out, forward, over = update_with(n - 1, (over,), False)

    def fetch_rest(rest):
        got = []
        for step in range(1 + deepest):
            got.append(travel([rest], got, step))
        own, cross = places(0)
        return tuple(pick([(among(m), array_at(k, [rest], got)) for k, m in found.items()]) for found in (own, cross))

    rest_own, rest_cross = lax.cond(over[0, 0] > 0.5, fetch_rest, lambda rest: (rest, rest), rest)
    return tuple(update_with(n, (rest_own, rest_cross, forward, out), True))


def solution(mesh):
    return jax.shard_map(
        on_device,
        mesh=mesh,
        in_specs=(P("rows", "cols", None, None), P("rows", "cols"), P(), P("rows", None, None)),
        out_specs=(P("rows", "cols", None, None), P("rows", None, None)),
        check_vma=False,
    )
```
